512 devices in a mesh: roll: 64 (over y_hi, z, core), tp: 8 (over x, y_lo).
Axes of the slice: x: 4, y: 8 (y_hi: 4, y_lo: 2; y = y_hi * 2 + y_lo), z: 8, core: 2. Of those that a mesh axis runs over, the one named last changes fastest.
Arguments:
- hidden: bfloat16 [4, 4096, 5120], P(None, ('roll', 'tp')), may hold values from -6 to 6
- queries: bfloat16 [4, 4096, 4096], P(None, 'roll', 'tp'), may hold values from -6 to 6
- key_cache: bfloat16 [4096, 32, 1024], P('roll', None, 'tp'), may hold values from -6 to 6
- value_cache: bfloat16 [4096, 32, 1024], P('roll', None, 'tp'), may hold values from -6 to 6
- cache_len: int32 [4096], P('roll'), may hold values from 2 to 32, as said below
- base_key: bfloat16 [5120, 1024], P(None, 'tp'), may hold values from -0.078125 to 0.078125
- base_value: bfloat16 [5120, 1024], P(None, 'tp'), may hold values from -0.078125 to 0.078125
- factor_a: bfloat16 [64, 2, 5120, 64], P('roll', None, 'tp'), may hold values from -0.078125 to 0.078125
- factor_b: bfloat16 [64, 2, 64, 1024], P('roll', None, None, 'tp'), may hold values from -0.375 to 0.375
- owner: int32 [2], replicated, may hold values from 0 to 63
Outputs:
- attended: bfloat16 [4, 4096, 4096], P(None, 'roll', 'tp')
The draws below stay inside these ranges and needn't reach their ends.
Inputs may be any that keep to these rules, and one draw needn't show every extreme that they name: `cache_len`: the first sample of each rollout group uses all 32 positions.
All inputs are finite; a program needn't handle non-finite values.
Results may differ from the reference program's by a relative error of at most 0.008.
Values may be sent and summed in bfloat16 or wider, within the bound.
A program may use at most 64 MiB of HBM per device.

```python
import math
import jax
import jax.numpy as jnp
from jax import lax

D = 5120
KVH = 8
HD = 128
QPK = 4
R = 64
STEPS = 4
SAMP = 64
CACHE = 32
SAMPLES = 4096
N_ROLL = 64


def draw_queries(key, part):
    key = jax.random.fold_in(key, 11)
    shape = (STEPS, SAMPLES, KVH * QPK * HD)
    values = jnp.clip(jax.random.normal(key, shape, jnp.float32), -6.0, 6.0)
    return values.astype(jnp.bfloat16)


def draw_key_cache(key, part):
    key = jax.random.fold_in(key, 12)
    shape = (SAMPLES, CACHE, KVH * HD)
    values = jnp.clip(jax.random.normal(key, shape, jnp.float32), -6.0, 6.0)
    return values.astype(jnp.bfloat16)


def draw_cache_len(key, part):
    key = jax.random.fold_in(key, 13)
    lengths = jax.random.randint(key, (SAMPLES,), 2, CACHE + 1, jnp.int32)
    return jnp.where(jnp.arange(SAMPLES) % SAMP == 0, CACHE, lengths).astype(jnp.int32)


def block_scale(rng, shape, pieces, smallest, largest):
    factor_of, own = 1.0, jax.random.fold_in(rng, 6)
    for position, blocks in pieces:
        steps = jnp.exp(jax.random.uniform(jax.random.fold_in(own, position), (blocks,), jnp.float32, smallest / len(pieces), largest / len(pieces)))
        factor_of = factor_of * jnp.repeat(steps, shape[position] // blocks).reshape([-1 if axis == position else 1 for axis in range(len(shape))])
    return factor_of


def noise(key, shape, scale, limit, cuts=(), dtype=jnp.bfloat16):
    entries = jax.random.normal(key, shape, jnp.float32) * scale
    if len(cuts) > 0:
        entries = block_scale(key, shape, cuts, -0.22, 0.18) * entries
    return jnp.clip(entries, min=-limit, max=limit).astype(dtype)


def setup_inputs(seed: int = 0) -> dict:
    keys = jax.random.split(jax.random.key(seed), 11)
    hidden = noise(keys[0], (STEPS, SAMPLES, D), 1.0, 6.0, ((1, 512),))
    queries = draw_queries(jax.random.fold_in(keys[10], 71), 0)
    key_cache = draw_key_cache(jax.random.fold_in(keys[10], 71), 0)
    value_cache = noise(keys[3], (SAMPLES, CACHE, KVH * HD), 1.0, 6.0, ((0, 64), (2, 8)))
    cache_len = draw_cache_len(jax.random.fold_in(keys[10], 71), 0)
    base_key = noise(keys[5], (D, KVH * HD), D ** -0.5, 0.078125, ((1, 8),))
    base_value = noise(keys[6], (D, KVH * HD), D ** -0.5, 0.078125, ((1, 8),))
    factor_a = noise(keys[7], (N_ROLL, 2, D, R), D ** -0.5, 0.078125, ((0, 64), (2, 8)))
    factor_b = noise(keys[8], (N_ROLL, 2, R, KVH * HD), (4 * R) ** -0.5, 0.375, ((0, 64), (3, 8)))
    owner = jax.random.randint(keys[9], (2,), 0, N_ROLL).astype(jnp.int32)
    return {"hidden": hidden, "queries": queries, "key_cache": key_cache, "value_cache": value_cache, "cache_len": cache_len, "base_key": base_key, "base_value": base_value, "factor_a": factor_a, "factor_b": factor_b, "owner": owner}


def reference(hidden, queries, key_cache, value_cache, cache_len, base_key, base_value, factor_a, factor_b, owner):
    merged = []
    for member, weights in ((0, base_key), (1, base_value)):
        update = jnp.dot(factor_a[owner[member], member], factor_b[owner[member], member], preferred_element_type=jnp.float32)
        merged.append((weights.astype(jnp.float32) + update).astype(jnp.bfloat16))
    token_rows = hidden.reshape(STEPS * SAMPLES, D)
    new_key = jnp.dot(token_rows, merged[0], preferred_element_type=jnp.float32).astype(jnp.bfloat16)
    new_value = jnp.dot(token_rows, merged[1], preferred_element_type=jnp.float32).astype(jnp.bfloat16)
    new_key = new_key.reshape(STEPS, SAMPLES, KVH, HD).astype(jnp.float32)
    new_value = new_value.reshape(STEPS, SAMPLES, KVH, HD).astype(jnp.float32)
    query_heads = queries.reshape(STEPS, SAMPLES, KVH, QPK, HD).astype(jnp.float32)
    cached_keys = key_cache.reshape(SAMPLES, CACHE, KVH, HD).astype(jnp.float32)
    cached_values = value_cache.reshape(SAMPLES, CACHE, KVH, HD).astype(jnp.float32)
    scale = 1.0 / math.sqrt(HD)
    cache_scores = jnp.einsum('tshjd,schd->tshjc', query_heads, cached_keys) * scale
    new_scores = jnp.einsum('tshjd,ushd->tshju', query_heads, new_key) * scale
    cache_mask = (jnp.arange(CACHE)[None, :] < cache_len[:, None])[None, :, None, None, :]
    new_mask = (jnp.arange(STEPS)[None, :] <= jnp.arange(STEPS)[:, None])[:, None, None, None, :]
    top = jnp.maximum(lax.optimization_barrier(jnp.max(jnp.where(cache_mask, cache_scores, -jnp.inf), axis=-1)), lax.optimization_barrier(jnp.max(jnp.where(new_mask, new_scores, -jnp.inf), axis=-1)))
    cache_weight = jnp.where(cache_mask, jnp.exp(cache_scores - top[..., None]), 0.0)
    new_weight = jnp.where(new_mask, jnp.exp(new_scores - top[..., None]), 0.0)
    total = lax.optimization_barrier(jnp.sum(cache_weight, axis=-1)) + lax.optimization_barrier(jnp.sum(new_weight, axis=-1))
    summed = jnp.einsum('tshjc,schd->tshjd', cache_weight, cached_values) + jnp.einsum('tshju,ushd->tshjd', new_weight, new_value)
    attended = summed / total[..., None]
    return attended.reshape(STEPS, SAMPLES, KVH * QPK * HD).astype(jnp.bfloat16)
```

```python
import functools
import math

import jax
import jax.numpy as jnp
from jax import lax
from jax.experimental import pallas as pl
from jax.experimental.pallas import tpu as pltpu
from jax.sharding import PartitionSpec as P

D = 5120
HD = 128
QPK = 4
R = 64
STEPS = 4
SAMP = 64
CACHE = 32
TP = 8
CHUNK = D // TP
NC = D // CHUNK
TOK = STEPS * SAMP // TP
CHIPS = 32
PIECES = 24
LANES = (CHUNK + HD) // 128
GROUP = 16
GROUPS = SAMP // GROUP
ROWS = STEPS * QPK * GROUP
NEG = -1e30
MESH = pl.DeviceIdType.MESH
NT = (((1,), (1,)), ((), ()))


def kernel(
    owner, lens, hidden, queries, keys, values, base_key, base_value, down, up, out,
    gathered, weights, kbuf, vbuf, half, other, bins, full, acc, top_ref, sum_ref,
    low_part, low_bins, low_all,
    load_sem, p0_send, p0_recv, p1_send, p1_recv, p2_send, p2_recv, p3_send, p3_recv,
    h_send, h_recv, l_send, l_recv, g_send, g_recv,
):
    roll, tp = lax.axis_index("roll"), lax.axis_index("tp")
    chip, core = roll // 2, roll % 2
    x, y = tp // 2, tp % 2
    pos = lambda px, py: lax.rem(px + 8, 4) * 2 + py
    right, left, across = pos(x + 1, y), pos(x - 1, y), pos(x, 1 - y)

    def remote(src, dst, send, recv, to_roll, to_tp):
        return pltpu.make_async_remote_copy(
            src_ref=src, dst_ref=dst, send_sem=send, recv_sem=recv,
            device_id=(to_roll, to_tp), device_id_type=MESH,
        )

    loads = [
        pltpu.make_async_copy(base_key, weights.at[:, pl.ds(0, HD)], load_sem.at[0]),
        pltpu.make_async_copy(base_value, weights.at[:, pl.ds(HD, HD)], load_sem.at[1]),
        pltpu.make_async_copy(keys, kbuf, load_sem.at[2]),
        pltpu.make_async_copy(values, vbuf, load_sem.at[3]),
    ]
    for c in range(NC):
        loads.append(
            pltpu.make_async_copy(
                hidden.at[:, pl.ds(c * CHUNK, CHUNK)], gathered.at[c, tp], load_sem.at[4 + c]
            )
        )
    for copy in loads:
        copy.start()

    barrier = pltpu.get_barrier_semaphore()

    def greet_tp(d, _):
        pl.semaphore_signal(barrier, inc=1, device_id=(roll, lax.rem(tp + d, TP)), device_id_type=MESH)
        return 0

    def greet_roll(d, _):
        to = lax.rem(chip + d, CHIPS) * 2 + core
        pl.semaphore_signal(barrier, inc=1, device_id=(to, tp), device_id_type=MESH)
        return 0

    pl.semaphore_signal(barrier, inc=1, device_id=(chip * 2 + 1 - core, tp), device_id_type=MESH)
    lax.fori_loop(1, TP, greet_tp, 0)
    lax.fori_loop(1, CHIPS, greet_roll, 0)
    pl.semaphore_wait(barrier, 1 + TP - 1 + CHIPS - 1)

    twin = chip * 2 + 1 - core
    mine = pl.ds(pl.multiple_of(core * R, R), R)
    theirs = pl.ds(pl.multiple_of((1 - core) * R, R), R)
    p0 = [
        remote(down.at[theirs], other.at[:, pl.ds(0, CHUNK)], p0_send.at[0], p0_recv.at[0], twin, tp),
        remote(up.at[theirs], other.at[:, pl.ds(CHUNK, HD)], p0_send.at[1], p0_recv.at[1], twin, tp),
    ]
    for copy in p0:
        copy.start()

    def hop(c, kind, block, to, src=None, rows=None):
        dst = gathered.at[c, block]
        if rows is not None:
            dst = dst.at[rows]
        return remote(dst if src is None else src, dst, h_send.at[c, kind], h_recv.at[c, kind], roll, to)

    sends = []

    def start(copy):
        copy.start()
        sends.append(copy)

    for c in range(NC):
        own = hidden.at[:, pl.ds(c * CHUNK, CHUNK)]
        start(hop(c, 0, tp, across, own))
        start(hop(c, 1, tp, right, own))
        start(hop(c, 2, tp, left, own))

    def landed(c, kind, block, rows=None):
        hop(c, kind, block, across, rows=rows).wait_recv()

    top_rows, low_rows = pl.ds(0, TOK // 2), pl.ds(TOK // 2, TOK // 2)
    far, far_across = pos(x + 2, y), pos(x + 2, 1 - y)

    def spread(c):
        landed(c, 0, across)
        start(hop(c, 3, across, right))
        start(hop(c, 4, across, left))
        landed(c, 1, left)
        start(hop(c, 5, left, right, rows=top_rows))
        landed(c, 2, right)
        start(hop(c, 6, right, left, rows=low_rows))

    def spread_again(c):
        landed(c, 3, pos(x - 1, 1 - y))
        start(hop(c, 7, pos(x - 1, 1 - y), right, rows=top_rows))
        landed(c, 4, pos(x + 1, 1 - y))
        start(hop(c, 8, pos(x + 1, 1 - y), left, rows=low_rows))

    def complete(c):
        landed(c, 5, far, top_rows)
        landed(c, 6, far, low_rows)
        landed(c, 7, far_across, top_rows)
        landed(c, 8, far_across, low_rows)
        loads[4 + c].wait()

    scale = 1.0 / math.sqrt(HD)
    row = lax.broadcasted_iota(jnp.int32, (QPK * GROUP, GROUP * CACHE), 0)
    col = lax.broadcasted_iota(jnp.int32, (QPK * GROUP, GROUP * CACHE), 1)
    same = (row % GROUP) == (col // CACHE)
    col_row = lax.broadcasted_iota(jnp.int32, (1, GROUP * CACHE), 1)

    def block_queries(g, t):
        at = pl.ds(pl.multiple_of(g * GROUP, GROUP), GROUP)
        return jnp.concatenate([queries[t, at, j * HD : (j + 1) * HD] for j in range(QPK)], axis=0)

    def cached(g, _):
        at = pl.ds(pl.multiple_of(g * GROUP, GROUP), GROUP)
        k = kbuf[at].reshape(GROUP * CACHE, HD)
        v = vbuf[at].reshape(GROUP * CACHE, HD)
        length = jnp.zeros((1, GROUP * CACHE), jnp.int32)
        for s in range(GROUP):
            length = jnp.where(col_row // CACHE == s, lens[g * GROUP + s], length)
        live = same & (col_row % CACHE < length)
        for t in range(STEPS):
            q = block_queries(g, t)
            scores = lax.dot_general(q, k, NT, preferred_element_type=jnp.float32) * scale
            scores = jnp.where(live, scores, NEG)
            top = jnp.max(scores, axis=1, keepdims=True)
            w = jnp.exp(scores - top)
            total = jnp.sum(w, axis=1, keepdims=True)
            mixed = jnp.dot(w.astype(jnp.bfloat16), v, preferred_element_type=jnp.float32)
            to = pl.ds(t * QPK * GROUP, QPK * GROUP)
            acc[g, to] = mixed
            top_ref[g, to] = jnp.broadcast_to(top, (QPK * GROUP, HD))
            sum_ref[g, to] = jnp.broadcast_to(total, (QPK * GROUP, HD))
        return 0

    for copy in p0:
        copy.wait_recv()
    owner_here = owner[core]
    owner_chip, owner_core = owner_here // 2, owner_here % 2
    for b in range(LANES):
        if b < LANES - 1:
            own = down[mine, b * 128 : (b + 1) * 128]
        else:
            own = up[mine, :]
        kept = jnp.where(owner_core == core, own, other[:, b * 128 : (b + 1) * 128])
        half[b * 4 : b * 4 + 4] = kept.reshape(4, 16, 128)

    def piece_to(k):
        return remote(half.at[k], bins.at[chip], p1_send.at[k], p1_recv.at[chip], k * 2 + core, tp)

    def piece_from(k):
        return remote(half.at[0], bins.at[k], p1_send.at[0], p1_recv.at[k], k * 2 + core, tp)

    def send_piece(d, _):
        k = lax.rem(chip + d, CHIPS)

        @pl.when(k < PIECES)
        def _():
            piece_to(k).start()

        return 0

    lax.fori_loop(1, CHIPS, send_piece, 0)

    loads[2].wait()
    loads[3].wait()
    lax.fori_loop(0, 1, cached, 0)

    def spread_to(k):
        return remote(full.at[core, chip], full.at[core, chip], p2_send.at[k], p2_recv.at[chip], k * 2 + core, tp)

    @pl.when(chip < PIECES)
    def _():
        bins[chip] = half[chip]

        def wait_piece(d, _):
            piece_from(lax.rem(chip + d, CHIPS)).wait_recv()
            return 0

        lax.fori_loop(1, CHIPS, wait_piece, 0)
        full[core, chip] = bins[owner_chip]

        def send_out(d, _):
            spread_to(lax.rem(chip + d, CHIPS)).start()
            return 0

        lax.fori_loop(1, CHIPS, send_out, 0)

    lax.fori_loop(1, 2, cached, 0)
    spread(0)
    spread(1)

    def wait_out(d, _):
        k = lax.rem(chip + d, CHIPS)

        @pl.when(k < PIECES)
        def _():
            remote(half.at[0], full.at[core, k], p2_send.at[0], p2_recv.at[k], k * 2 + core, tp).wait_recv()

        return 0

    lax.fori_loop(1, CHIPS, wait_out, 0)

    p3 = remote(full.at[core], full.at[core], p3_send, p3_recv, twin, tp)
    p3.start()

    spread_again(0)
    lax.fori_loop(2, 3, cached, 0)
    spread(2)
    spread_again(1)
    lax.fori_loop(3, 4, cached, 0)
    loads[0].wait()
    loads[1].wait()

    projected = None
    for c in range(NC):
        if c + 3 < NC:
            spread(c + 3)
        if c + 2 < NC:
            spread_again(c + 2)
        complete(c)
        part = jnp.dot(
            gathered[c].reshape(TP * TOK, CHUNK), weights[c * CHUNK : (c + 1) * CHUNK],
            preferred_element_type=jnp.float32,
        )
        projected = part if projected is None else projected + part

    remote(full.at[1 - core], full.at[1 - core], p3_send, p3_recv, twin, tp).wait_recv()
    down_now = jnp.concatenate(
        [full[:, b * 4 : b * 4 + 4].reshape(2 * R, 128) for b in range(LANES - 1)], axis=1
    )
    up_now = full[:, 4 * LANES - 4 : 4 * LANES].reshape(2 * R, HD)
    low_part[...] = lax.dot_general(
        gathered[tp].reshape(TP * TOK, CHUNK), down_now, NT, preferred_element_type=jnp.float32
    ).reshape(TP, TOK, 2 * R)

    def low_to(d):
        q = lax.rem(tp + d, TP)
        return remote(low_part.at[q], low_bins.at[tp], l_send.at[q], l_recv.at[tp], roll, q)

    def low_from(d):
        q = lax.rem(tp + d, TP)
        return remote(low_part.at[q], low_bins.at[q], l_send.at[q], l_recv.at[q], roll, q)

    def all_to(d):
        q = lax.rem(tp + d, TP)
        return remote(low_all.at[tp], low_all.at[tp], g_send.at[q], g_recv.at[tp], roll, q)

    def all_from(d):
        q = lax.rem(tp + d, TP)
        return remote(low_all.at[q], low_all.at[q], g_send.at[q], g_recv.at[q], roll, q)

    for d in range(1, TP):
        low_to(d).start()
    low_bins[tp] = low_part[tp]
    for d in range(1, TP):
        low_from(d).wait_recv()
    low_all[tp] = jnp.sum(low_bins[...], axis=0)
    for d in range(1, TP):
        all_to(d).start()
    for d in range(1, TP):
        all_from(d).wait_recv()

    low = low_all[...].reshape(TP * TOK, 2 * R)
    low_high = low.astype(jnp.bfloat16)
    low_rest = (low - low_high.astype(jnp.float32)).astype(jnp.bfloat16)
    zero = jnp.zeros((R, HD), jnp.bfloat16)
    up_both = jnp.concatenate(
        [jnp.concatenate([up_now[:R], zero], axis=0), jnp.concatenate([zero, up_now[R:]], axis=0)], axis=1
    )
    projected = projected + (
        jnp.dot(low_high, up_both, preferred_element_type=jnp.float32)
        + jnp.dot(low_rest, up_both, preferred_element_type=jnp.float32)
    )
    fresh = projected.astype(jnp.bfloat16)

    span = GROUP * STEPS
    row2 = lax.broadcasted_iota(jnp.int32, (ROWS, span), 0)
    col2 = lax.broadcasted_iota(jnp.int32, (ROWS, span), 1)
    sample2 = col2 // TOK * (GROUP // 2) + col2 % (GROUP // 2)
    step2 = col2 % TOK // (GROUP // 2)
    live2 = (row2 % GROUP == sample2) & (step2 <= row2 // (QPK * GROUP))
    for g in range(GROUPS):
        q = jnp.concatenate([block_queries(g, t) for t in range(STEPS)], axis=0)
        k = fresh[g * span : (g + 1) * span, :HD]
        v = fresh[g * span : (g + 1) * span, HD:]
        scores = lax.dot_general(q, k, NT, preferred_element_type=jnp.float32) * scale
        scores = jnp.where(live2, scores, NEG)
        old_top = top_ref[g]
        top = jnp.maximum(old_top, jnp.max(scores, axis=1, keepdims=True))
        w = jnp.exp(scores - top[:, :span])
        fade = jnp.exp(old_top - top)
        total = sum_ref[g] * fade + jnp.sum(w, axis=1, keepdims=True)
        mixed = acc[g] * fade + jnp.dot(w.astype(jnp.bfloat16), v, preferred_element_type=jnp.float32)
        done = (mixed / total).astype(jnp.bfloat16)
        for t in range(STEPS):
            for j in range(QPK):
                at = (t * QPK + j) * GROUP
                out[t, g * GROUP : (g + 1) * GROUP, j * HD : (j + 1) * HD] = done[at : at + GROUP]

    for copy in p0:
        copy.wait_send()
    p3.wait_send()
    for copy in sends:
        copy.wait_send()
    for d in range(1, TP):
        low_to(d).wait_send()
        all_to(d).wait_send()

    def sent_piece(d, _):
        k = lax.rem(chip + d, CHIPS)

        @pl.when(k < PIECES)
        def _():
            piece_to(k).wait_send()

        return 0

    lax.fori_loop(1, CHIPS, sent_piece, 0)

    @pl.when(chip < PIECES)
    def _():
        def sent_out(d, _):
            spread_to(lax.rem(chip + d, CHIPS)).wait_send()
            return 0

        lax.fori_loop(1, CHIPS, sent_out, 0)


def local(hidden, queries, key_cache, value_cache, cache_len, base_key, base_value, factor_a, factor_b, owner):
    down = jnp.swapaxes(factor_a[0], 1, 2).reshape(2 * R, CHUNK)
    up = factor_b[0].reshape(2 * R, HD)
    vmem = pl.BlockSpec(memory_space=pltpu.VMEM)
    smem = pl.BlockSpec(memory_space=pltpu.SMEM)
    hbm = pl.BlockSpec(memory_space=pl.ANY)
    dma = pltpu.SemaphoreType.DMA
    return pl.pallas_call(
        kernel,
        out_shape=jax.ShapeDtypeStruct((STEPS, SAMP, QPK * HD), jnp.bfloat16),
        in_specs=[smem, smem, hbm, vmem, hbm, hbm, hbm, hbm, vmem, vmem],
        out_specs=vmem,
        scratch_shapes=[
            pltpu.VMEM((NC, TP, TOK, CHUNK), jnp.bfloat16),
            pltpu.VMEM((D, 2 * HD), jnp.bfloat16),
            pltpu.VMEM((SAMP, CACHE, HD), jnp.bfloat16),
            pltpu.VMEM((SAMP, CACHE, HD), jnp.bfloat16),
            pltpu.VMEM((PIECES, 16, 128), jnp.bfloat16),
            pltpu.VMEM((R, CHUNK + HD), jnp.bfloat16),
            pltpu.VMEM((CHIPS, 16, 128), jnp.bfloat16),
            pltpu.VMEM((2, PIECES, 16, 128), jnp.bfloat16),
            pltpu.VMEM((GROUPS, ROWS, HD), jnp.float32),
            pltpu.VMEM((GROUPS, ROWS, HD), jnp.float32),
            pltpu.VMEM((GROUPS, ROWS, HD), jnp.float32),
            pltpu.VMEM((TP, TOK, 2 * R), jnp.float32),
            pltpu.VMEM((TP, TOK, 2 * R), jnp.float32),
            pltpu.VMEM((TP, TOK, 2 * R), jnp.float32),
            dma((4 + NC,)),
            dma((2,)), dma((2,)),
            dma((PIECES,)), dma((CHIPS,)),
            dma((CHIPS,)), dma((PIECES,)),
            dma, dma,
            dma((NC, 9)), dma((NC, 9)),
            dma((TP,)), dma((TP,)), dma((TP,)), dma((TP,)),
        ],
        compiler_params=pltpu.CompilerParams(
            collective_id=0, has_side_effects=True, vmem_limit_bytes=48 * 1024 * 1024
        ),
    )(
        owner, cache_len, hidden.reshape(STEPS * SAMP // TP, D), queries, key_cache, value_cache,
        base_key, base_value, down, up,
    )


def solution(mesh):
    placed = (
        P(None, ("roll", "tp"), None),
        P(None, "roll", "tp"),
        P("roll", None, "tp"),
        P("roll", None, "tp"),
        P("roll"),
        P(None, "tp"),
        P(None, "tp"),
        P("roll", None, "tp", None),
        P("roll", None, None, "tp"),
        P(),
    )
    return jax.shard_map(
        local, mesh=mesh, in_specs=placed, out_specs=P(None, "roll", "tp"), check_vma=False
    )
```

```python
import math

import jax
import jax.numpy as jnp
from jax import lax
from jax.experimental import pallas as pl
from jax.experimental.pallas import tpu as pltpu
from jax.sharding import PartitionSpec as P

D = 5120
HD = 128
QPK = 4
R = 64
STEPS = 4
SAMP = 64
CACHE = 32
TP = 8
ROWS_TP = D // TP
RANK = 2 * R // TP
NC = 4
CHUNK = D // NC
TOK = STEPS * SAMP // TP
CHIPS = 32
REDUCERS = 8
GROUP = 16
GROUPS = SAMP // GROUP
ROWS = STEPS * QPK * GROUP
NEG = -1e30
MESH = pl.DeviceIdType.MESH
NT = (((1,), (1,)), ((), ()))
TN = (((0,), (0,)), ((), ()))


def kernel(
    owner_hbm, lens_hbm, hidden, queries_hbm, keys, values, base_key, base_value, down_hbm, up_hbm, out,
    owner, lens, queries, down, up,
    gathered, weights, kbuf, vbuf, down_other, up_other, down_half, up_half, down_bins, up_bins, down_now, up_now,
    acc, top_ref, sum_ref, low_all,
    load_sem, p0_send, p0_recv, p1_send, p1_recv, p2_send, p2_recv, p3_send, p3_recv,
    h_send, h_recv, g_send, g_recv, go_sem,
):
    roll, tp = lax.axis_index("roll"), lax.axis_index("tp")
    y_hi, z, core = roll // 16, roll // 2 % 8, roll % 2
    chip = (z // 4) * 16 + y_hi * 4 + z % 4
    x, y = tp // 2, tp % 2
    pos = lambda px, py: lax.rem(px + 8, 4) * 2 + py
    def roll_of(k, c):
        return (k // 4 % 4) * 16 + ((k // 16) * 4 + k % 4) * 2 + c

    right, left, across = pos(x + 1, y), pos(x - 1, y), pos(x, 1 - y)
    twin = roll + 1 - 2 * core
    down_core = tp // 4
    has_down = core == down_core
    reduces = chip < REDUCERS
    late = chip >= CHIPS // 2
    partner = roll_of(lax.rem(chip + CHIPS // 2, CHIPS), core)
    picked = lax.rem(chip + TP - tp, TP)

    def remote(src, dst, send, recv, to_roll, to_tp):
        return pltpu.make_async_remote_copy(
            src_ref=src, dst_ref=dst, send_sem=send, recv_sem=recv,
            device_id=(to_roll, to_tp), device_id_type=MESH,
        )

    loads = [
        pltpu.make_async_copy(src, dst, load_sem.at[k])
        for k, (src, dst) in enumerate(
            [
                (down_hbm, down), (up_hbm, up), (owner_hbm, owner), (lens_hbm, lens), (queries_hbm, queries),
                (keys, kbuf), (values, vbuf),
                (base_key, weights.at[:, pl.ds(0, HD)]), (base_value, weights.at[:, pl.ds(HD, HD)]),
            ]
            + [(hidden.at[:, pl.ds(c * CHUNK, CHUNK)], gathered.at[c, tp]) for c in range(NC)]
        )
    ]
    for copy in loads:
        copy.start()

    barrier = pltpu.get_barrier_semaphore()

    def greet(to_roll, to_tp):
        pl.semaphore_signal(barrier, inc=1, device_id=(to_roll, to_tp), device_id_type=MESH)

    greet(twin, tp)

    def greet_tp(d, _):
        greet(roll, lax.rem(tp + d, TP))
        return 0

    lax.fori_loop(1, TP, greet_tp, 0)

    @pl.when(reduces)
    def _():
        def greet_sender(k, _):
            greet(roll_of(k, jnp.where(has_down, core, chip // 4)), jnp.where(has_down, picked, tp))
            return 0

        lax.fori_loop(CHIPS // 2, CHIPS, greet_sender, 0)

    @pl.when(jnp.logical_not(late))
    def _():
        greet(partner, tp)

    pl.semaphore_wait(barrier, jnp.where(late, TP + TP + 1, TP))

    @pl.when(late)
    def _():
        pl.semaphore_signal(go_sem, inc=1, device_id=(partner, tp), device_id_type=MESH)

    own_down = has_down & reduces & (picked == tp)
    own_up = (core != down_core) & reduces & (chip // 4 == core)
    mine = pl.ds(pl.multiple_of(core * R, R), R)
    theirs = pl.ds(pl.multiple_of((1 - core) * R, R), R)
    p0 = [
        remote(down_hbm.at[theirs], down_other, p0_send.at[0], p0_recv.at[0], twin, tp),
        remote(up_hbm.at[theirs], up_other, p0_send.at[1], p0_recv.at[1], twin, tp),
    ]
    for copy in p0:
        copy.start()
    for copy in loads[:3]:
        copy.wait()
    owner_core = owner[core] % 2
    for copy in p0:
        copy.wait_recv()
    down_half[...] = jnp.where(owner_core == core, down[mine, :], down_other[...]).reshape(4, RANK, ROWS_TP)
    up_half[...] = jnp.where(owner_core == core, up[mine, :], up_other[...]).reshape(4, RANK, HD)

    def down_to(a):
        return remote(
            down_half.at[a], down_bins.at[chip], p1_send.at[a], p1_recv.at[chip],
            roll_of(lax.rem(tp + 4 * core + a, TP), core), 4 * core + a,
        )

    def up_to(a):
        return remote(
            up_half.at[a], up_bins.at[chip], p1_send.at[4 + a], p1_recv.at[chip], roll_of(4 * core + a, 1 - down_core), tp
        )

    def is_own_down(a):
        return own_down & (4 * core + a == tp)

    def is_own_up(a):
        return own_up & (4 * core + a == chip)

    def send_pieces():
        for a in range(4):
            @pl.when(jnp.logical_not(is_own_down(a)))
            def _():
                down_to(a).start()

            @pl.when(jnp.logical_not(is_own_up(a)))
            def _():
                up_to(a).start()

            @pl.when(is_own_down(a))
            def _():
                down_bins[chip] = down_half[a]

            @pl.when(is_own_up(a))
            def _():
                up_bins[chip] = up_half[a]

    def hop(c, kind, block, to, src=None, rows=None):
        dst = gathered.at[c, block]
        if rows is not None:
            dst = dst.at[rows]
        return remote(dst if src is None else src, dst, h_send.at[c, kind], h_recv.at[c, kind], roll, to)

    sends = []

    def start(copy):
        copy.start()
        sends.append(copy)

    def landed(c, kind, block, rows=None):
        hop(c, kind, block, across, rows=rows).wait_recv()

    top_rows, low_rows = pl.ds(0, TOK // 2), pl.ds(TOK // 2, TOK // 2)
    far, far_across = pos(x + 2, y), pos(x + 2, 1 - y)
    left_across, right_across = pos(x - 1, 1 - y), pos(x + 1, 1 - y)
    along_y = (0, 1)
    along_x = (2, 3)

    def pass_on(c):
        landed(c, 1, left)
        start(hop(c, 5, left, right, rows=top_rows))
        if c in along_x:
            start(hop(c, 3, left, across))
        landed(c, 2, right)
        start(hop(c, 6, right, left, rows=low_rows))
        if c in along_x:
            start(hop(c, 4, right, across))

    def spread(c):
        landed(c, 0, across)
        start(hop(c, 3, across, right))
        start(hop(c, 4, across, left))
        pass_on(c)

    def spread_again(c):
        landed(c, 3, left_across)
        start(hop(c, 7, left_across, right, rows=top_rows))
        landed(c, 4, right_across)
        start(hop(c, 8, right_across, left, rows=low_rows))

    def far_across_y(c):
        landed(c, 5, far, top_rows)
        landed(c, 6, far, low_rows)
        start(hop(c, 7, far, across))

    scale = 1.0 / math.sqrt(HD)
    row = lax.broadcasted_iota(jnp.int32, (QPK * GROUP, GROUP * CACHE), 0)
    col = lax.broadcasted_iota(jnp.int32, (QPK * GROUP, GROUP * CACHE), 1)
    same = (row % GROUP) == (col // CACHE)
    col_row = lax.broadcasted_iota(jnp.int32, (1, GROUP * CACHE), 1)

    def block_queries(g, t):
        at = pl.ds(pl.multiple_of(g * GROUP, GROUP), GROUP)
        return jnp.concatenate([queries[t, at, j * HD : (j + 1) * HD] for j in range(QPK)], axis=0)

    def cached(g, _):
        at = pl.ds(pl.multiple_of(g * GROUP, GROUP), GROUP)
        k = kbuf[at].reshape(GROUP * CACHE, HD)
        v = vbuf[at].reshape(GROUP * CACHE, HD)
        length = jnp.zeros((1, GROUP * CACHE), jnp.int32)
        for s in range(GROUP):
            length = jnp.where(col_row // CACHE == s, lens[g * GROUP + s], length)
        live = same & (col_row % CACHE < length)
        for t in range(STEPS):
            q = block_queries(g, t)
            scores = lax.dot_general(q, k, NT, preferred_element_type=jnp.float32) * scale
            scores = jnp.where(live, scores, NEG)
            top = jnp.max(scores, axis=1, keepdims=True)
            w = jnp.exp(scores - top)
            total = jnp.sum(w, axis=1, keepdims=True)
            mixed = jnp.dot(w.astype(jnp.bfloat16), v, preferred_element_type=jnp.float32)
            to = pl.ds(t * QPK * GROUP, QPK * GROUP)
            acc[g, to] = mixed
            top_ref[g, to] = jnp.broadcast_to(top, (QPK * GROUP, HD))
            sum_ref[g, to] = jnp.broadcast_to(total, (QPK * GROUP, HD))
        return 0

    @pl.when(late)
    def _():
        send_pieces()

    for copy in loads[3:7]:
        copy.wait()
    lax.fori_loop(0, jnp.where(late, GROUPS, 0), cached, 0)
    for c in along_x + along_y:
        own = hidden.at[:, pl.ds(c * CHUNK, CHUNK)]
        start(hop(c, 0, tp, across, own))
        start(hop(c, 1, tp, right, own))
        start(hop(c, 2, tp, left, own))

    lax.fori_loop(jnp.where(late, GROUPS, 0), GROUPS, cached, 0)
    for c in along_x:
        pass_on(c)
    for c in along_y:
        spread(c)

    @pl.when(jnp.logical_not(late))
    def _():
        pl.semaphore_wait(go_sem, 1)
        send_pieces()

    for c in along_x:
        far_across_y(c)
    for c in along_y:
        spread_again(c)

    for copy in loads[7:]:
        copy.wait()
    projected = None
    for c in along_y + along_x:
        if c in along_y:
            landed(c, 5, far, top_rows)
            landed(c, 6, far, low_rows)
            landed(c, 7, far_across, top_rows)
            landed(c, 8, far_across, low_rows)
        else:
            landed(c, 0, across)
            landed(c, 3, left_across)
            landed(c, 4, right_across)
            landed(c, 7, far_across)
        part = jnp.dot(
            gathered[c].reshape(TP * TOK, CHUNK), weights[c * CHUNK : (c + 1) * CHUNK],
            preferred_element_type=jnp.float32,
        )
        projected = part if projected is None else projected + part

    def down_out(k):
        return remote(down_now.at[picked], down_now.at[picked], p2_send.at[k], p2_recv.at[picked], roll_of(k, core), tp)

    def up_out(k):
        return remote(up_now.at[chip], up_now.at[chip], p2_send.at[k], p2_recv.at[chip], roll_of(k, core), tp)

    @pl.when(reduces & has_down)
    def _():
        def wait_piece(k, _):
            @pl.when((k != chip) | (tp != picked))
            def _():
                remote(down_half.at[0], down_bins.at[k], p1_send.at[0], p1_recv.at[k], twin, tp).wait_recv()

            return 0

        lax.fori_loop(0, CHIPS, wait_piece, 0)
        source = owner[core] // 2
        down_now[picked] = down_bins[(source % 8) // 4 * 16 + source // 8 * 4 + source % 4]

        def send_out(k, _):
            @pl.when(k != chip)
            def _():
                down_out(k).start()

            return 0

        lax.fori_loop(0, CHIPS, send_out, 0)

    @pl.when(reduces & (core != down_core))
    def _():
        def wait_piece(k, _):
            @pl.when((k != chip) | (chip // 4 != core))
            def _():
                remote(up_half.at[0], up_bins.at[k], p1_send.at[4], p1_recv.at[k], twin, tp).wait_recv()

            return 0

        lax.fori_loop(0, CHIPS, wait_piece, 0)
        source = owner[chip // 4] // 2
        up_now[chip] = up_bins[(source % 8) // 4 * 16 + source // 8 * 4 + source % 4]

        def send_out(k, _):
            @pl.when(k != chip)
            def _():
                up_out(k).start()

            return 0

        lax.fori_loop(0, CHIPS, send_out, 0)

    p3_down = remote(down_now, down_now, p3_send, p3_recv, twin, tp)
    p3_up = remote(up_now, up_now, p3_send, p3_recv, twin, tp)

    @pl.when(has_down)
    def _():
        for k in range(REDUCERS):
            @pl.when((k != picked) | (chip >= REDUCERS))
            def _():
                remote(down_half.at[0], down_now.at[k], p1_send.at[0], p2_recv.at[k], twin, tp).wait_recv()
        p3_down.start()
        p3_up.wait_recv()

    @pl.when(core != down_core)
    def _():
        for k in range(REDUCERS):
            @pl.when(k != chip)
            def _():
                remote(up_half.at[0], up_now.at[k], p1_send.at[4], p2_recv.at[k], twin, tp).wait_recv()
        p3_up.start()
        p3_down.wait_recv()

    low = None
    for c in range(NC):
        rows = jnp.concatenate(
            [down_now[k] for k in range(c * CHUNK // ROWS_TP, (c + 1) * CHUNK // ROWS_TP)], axis=1
        )
        part = lax.dot_general(
            rows, gathered[c].reshape(TP * TOK, CHUNK), NT, preferred_element_type=jnp.float32
        )
        low = part if low is None else low + part
    low_all[tp] = low.astype(jnp.bfloat16)

    def all_to(d):
        q = lax.rem(tp + d, TP)
        return remote(low_all.at[tp], low_all.at[tp], g_send.at[q], g_recv.at[tp], roll, q)

    def all_from(d):
        q = lax.rem(tp + d, TP)
        return remote(low_all.at[q], low_all.at[q], g_send.at[q], g_recv.at[q], roll, q)

    for d in range(1, TP):
        all_to(d).start()
    zero = jnp.zeros((R, HD), jnp.bfloat16)
    up_rows = up_now[...].reshape(2 * R, HD)
    up_both = jnp.concatenate(
        [jnp.concatenate([up_rows[:R], zero], axis=0), jnp.concatenate([zero, up_rows[R:]], axis=0)], axis=1
    )
    for d in range(1, TP):
        all_from(d).wait_recv()
    projected = projected + lax.dot_general(
        low_all[...].reshape(2 * R, TP * TOK), up_both, TN, preferred_element_type=jnp.float32
    )
    fresh = projected.astype(jnp.bfloat16)

    span = GROUP * STEPS
    row2 = lax.broadcasted_iota(jnp.int32, (ROWS, span), 0)
    col2 = lax.broadcasted_iota(jnp.int32, (ROWS, span), 1)
    sample2 = col2 // TOK * (GROUP // 2) + col2 % (GROUP // 2)
    step2 = col2 % TOK // (GROUP // 2)
    live2 = (row2 % GROUP == sample2) & (step2 <= row2 // (QPK * GROUP))
    for g in range(GROUPS):
        q = jnp.concatenate([block_queries(g, t) for t in range(STEPS)], axis=0)
        k = fresh[g * span : (g + 1) * span, :HD]
        v = fresh[g * span : (g + 1) * span, HD:]
        scores = lax.dot_general(q, k, NT, preferred_element_type=jnp.float32) * scale
        scores = jnp.where(live2, scores, NEG)
        old_top = top_ref[g]
        top = jnp.maximum(old_top, jnp.max(scores, axis=1, keepdims=True))
        w = jnp.exp(scores - top[:, :span])
        fade = jnp.exp(old_top - top)
        total = sum_ref[g] * fade + jnp.sum(w, axis=1, keepdims=True)
        mixed = acc[g] * fade + jnp.dot(w.astype(jnp.bfloat16), v, preferred_element_type=jnp.float32)
        done = (mixed / total).astype(jnp.bfloat16)
        for t in range(STEPS):
            for j in range(QPK):
                at = (t * QPK + j) * GROUP
                out[t, g * GROUP : (g + 1) * GROUP, j * HD : (j + 1) * HD] = done[at : at + GROUP]

    for copy in p0 + sends:
        copy.wait_send()
    for d in range(1, TP):
        all_to(d).wait_send()
    for a in range(4):
        @pl.when(jnp.logical_not(is_own_down(a)))
        def _():
            down_to(a).wait_send()

        @pl.when(jnp.logical_not(is_own_up(a)))
        def _():
            up_to(a).wait_send()

    @pl.when(has_down)
    def _():
        p3_down.wait_send()

    @pl.when(core != down_core)
    def _():
        p3_up.wait_send()

    @pl.when(reduces & has_down)
    def _():
        def sent_out(d, _):
            down_out(lax.rem(chip + d, CHIPS)).wait_send()
            return 0

        lax.fori_loop(1, CHIPS, sent_out, 0)

    @pl.when(reduces & (core != down_core))
    def _():
        def sent_out(d, _):
            up_out(lax.rem(chip + d, CHIPS)).wait_send()
            return 0

        lax.fori_loop(1, CHIPS, sent_out, 0)


def local(hidden, queries, key_cache, value_cache, cache_len, base_key, base_value, factor_a, factor_b, owner):
    down = jnp.swapaxes(factor_a[0], 1, 2).reshape(2 * R, ROWS_TP)
    up = factor_b[0].reshape(2 * R, HD)
    hbm = pl.BlockSpec(memory_space=pltpu.HBM)
    dma = pltpu.SemaphoreType.DMA
    vmem, bf16, f32 = pltpu.VMEM, jnp.bfloat16, jnp.float32
    return pl.pallas_call(
        kernel,
        out_shape=jax.ShapeDtypeStruct((STEPS, SAMP, QPK * HD), jnp.bfloat16),
        in_specs=[hbm] * 10,
        out_specs=pl.BlockSpec(memory_space=pltpu.VMEM),
        scratch_shapes=[
            pltpu.SMEM((2,), jnp.int32),
            pltpu.SMEM((SAMP,), jnp.int32),
            vmem((STEPS, SAMP, QPK * HD), bf16),
            vmem((2 * R, ROWS_TP), bf16),
            vmem((2 * R, HD), bf16),
            vmem((NC, TP, TOK, CHUNK), bf16),
            vmem((D, 2 * HD), bf16),
            vmem((SAMP, CACHE, HD), bf16),
            vmem((SAMP, CACHE, HD), bf16),
            vmem((R, ROWS_TP), bf16),
            vmem((R, HD), bf16),
            vmem((4, RANK, ROWS_TP), bf16),
            vmem((4, RANK, HD), bf16),
            vmem((CHIPS, RANK, ROWS_TP), bf16),
            vmem((CHIPS, RANK, HD), bf16),
            vmem((REDUCERS, RANK, ROWS_TP), bf16),
            vmem((REDUCERS, RANK, HD), bf16),
            vmem((GROUPS, ROWS, HD), f32),
            vmem((GROUPS, ROWS, HD), f32),
            vmem((GROUPS, ROWS, HD), f32),
            vmem((TP, RANK, TP * TOK), bf16),
            dma((9 + NC,)),
            dma((2,)), dma((2,)),
            dma((8,)), dma((CHIPS,)),
            dma((CHIPS,)), dma((REDUCERS,)),
            dma, dma,
            dma((NC, 9)), dma((NC, 9)),
            dma((TP,)), dma((TP,)),
            pltpu.SemaphoreType.REGULAR,
        ],
        compiler_params=pltpu.CompilerParams(
            collective_id=0, has_side_effects=True, vmem_limit_bytes=63 * 1024 * 1024
        ),
    )(
        owner, cache_len, hidden.reshape(TOK, D), queries, key_cache, value_cache,
        base_key, base_value, down, up,
    )


def solution(mesh):
    placed = (
        P(None, ("roll", "tp"), None),
        P(None, "roll", "tp"),
        P("roll", None, "tp"),
        P("roll", None, "tp"),
        P("roll"),
        P(None, "tp"),
        P(None, "tp"),
        P("roll", None, "tp", None),
        P("roll", None, None, "tp"),
        P(),
    )
    return jax.shard_map(
        local, mesh=mesh, in_specs=placed, out_specs=P(None, "roll", "tp"), check_vma=False
    )
```

```python
import math

import jax
import jax.numpy as jnp
from jax import lax
from jax.experimental import pallas as pl
from jax.experimental.pallas import tpu as pltpu
from jax.sharding import PartitionSpec as P

D = 5120
HD = 128
QPK = 4
R = 64
STEPS = 4
SAMP = 64
CACHE = 32
TP = 8
ROWS_TP = D // TP
PIECE = 16
WIDTH = ROWS_TP + HD
NC = 4
CHUNK = D // NC
TOK = STEPS * SAMP // TP
ZS = 8
PICKERS = 4
YS = 4
GROUP = 16
GROUPS = SAMP // GROUP
ROWS = STEPS * QPK * GROUP
NEG = -1e30
MESH = pl.DeviceIdType.MESH
NT = (((1,), (1,)), ((), ()))
TN = (((0,), (0,)), ((), ()))


def kernel(
    owner_hbm, lens_hbm, hidden, queries_hbm, keys, values, base_key, base_value, down_hbm, up_hbm, out,
    owner, lens, queries, down, up,
    gathered, weights, kbuf, vbuf, other, half, bins_z, bins_y, now, acc, top_ref, sum_ref, low_all,
    load_sem, p0_send, p0_recv, p1_send, p1_recv, p2_send, p2_recv, p3_send, p3_recv, p4_send, p4_recv,
    h_send, h_recv, g_send, g_recv,
):
    roll, tp = lax.axis_index("roll"), lax.axis_index("tp")
    y_hi, z, core = roll // 16, roll // 2 % 8, roll % 2
    x, y = tp // 2, tp % 2
    pos = lambda px, py: lax.rem(px + 8, 4) * 2 + py
    right, left, across = pos(x + 1, y), pos(x - 1, y), pos(x, 1 - y)
    twin = roll + 1 - 2 * core
    picks = z < PICKERS

    def at_z(to_z):
        return y_hi * 16 + to_z * 2 + core

    def at_y(to_y):
        return to_y * 16 + z * 2 + core

    def remote(src, dst, send, recv, to_roll, to_tp):
        return pltpu.make_async_remote_copy(
            src_ref=src, dst_ref=dst, send_sem=send, recv_sem=recv,
            device_id=(to_roll, to_tp), device_id_type=MESH,
        )

    loads = [
        pltpu.make_async_copy(src, dst, load_sem.at[k])
        for k, (src, dst) in enumerate(
            [
                (down_hbm, down), (up_hbm, up), (owner_hbm, owner), (lens_hbm, lens), (queries_hbm, queries),
                (keys, kbuf), (values, vbuf),
                (base_key, weights.at[:, pl.ds(0, HD)]), (base_value, weights.at[:, pl.ds(HD, HD)]),
            ]
            + [(hidden.at[:, pl.ds(c * CHUNK, CHUNK)], gathered.at[c, tp]) for c in range(NC)]
        )
    ]
    for copy in loads:
        copy.start()

    barrier = pltpu.get_barrier_semaphore()

    def greet(to_roll, to_tp):
        pl.semaphore_signal(barrier, inc=1, device_id=(to_roll, to_tp), device_id_type=MESH)

    greet(twin, tp)
    for d in range(1, TP):
        greet(roll, lax.rem(tp + d, TP))

    @pl.when(picks)
    def _():
        for d in range(1, ZS):
            greet(at_z(lax.rem(z + d, ZS)), tp)
        for d in range(1, YS):
            greet(at_y(lax.rem(y_hi + d, YS)), tp)

    pl.semaphore_wait(barrier, jnp.where(picks, TP + PICKERS - 1 + YS - 1, TP + PICKERS))

    mine = pl.ds(pl.multiple_of(core * R, R), R)
    theirs = pl.ds(pl.multiple_of((1 - core) * R, R), R)
    p0 = [
        remote(down_hbm.at[theirs], other.at[:, pl.ds(0, ROWS_TP)], p0_send.at[0], p0_recv.at[0], twin, tp),
        remote(up_hbm.at[theirs], other.at[:, pl.ds(ROWS_TP, HD)], p0_send.at[1], p0_recv.at[1], twin, tp),
    ]
    for copy in p0:
        copy.start()
    for copy in loads[:3]:
        copy.wait()
    owner_here = owner[core]
    for copy in p0:
        copy.wait_recv()
    kept = jnp.where(
        owner_here % 2 == core, jnp.concatenate([down[mine, :], up[mine, :]], axis=1), other[...]
    )
    half[...] = kept.reshape(PICKERS, PIECE, WIDTH)

    def to_picker(a):
        return remote(half.at[a], bins_z.at[z], p1_send.at[a], p1_recv.at[z], at_z(a), tp)

    for a in range(PICKERS):
        @pl.when(z != a)
        def _():
            to_picker(a).start()

        @pl.when(z == a)
        def _():
            bins_z[z] = half[a]

    def to_other_y(k):
        return remote(bins_y.at[y_hi], bins_y.at[y_hi], p2_send.at[k], p2_recv.at[y_hi], at_y(k), tp)

    def pick_z():
        for d in range(1, ZS):
            k = lax.rem(z + d, ZS)
            remote(half.at[0], bins_z.at[k], p1_send.at[0], p1_recv.at[k], twin, tp).wait_recv()
        bins_y[y_hi] = bins_z[owner_here // 2 % ZS]
        for d in range(1, YS):
            to_other_y(lax.rem(y_hi + d, YS)).start()

    def to_column(k):
        return remote(now.at[core, z], now.at[core, z], p3_send.at[k], p3_recv.at[z], at_z(k), tp)

    def pick_y():
        for d in range(1, YS):
            k = lax.rem(y_hi + d, YS)
            remote(half.at[0], bins_y.at[k], p2_send.at[0], p2_recv.at[k], twin, tp).wait_recv()
        now[core, z] = bins_y[owner_here // 16]
        for k in range(ZS):
            @pl.when(z != k)
            def _():
                to_column(k).start()

    def hop(c, kind, block, to, src=None, rows=None):
        dst = gathered.at[c, block]
        if rows is not None:
            dst = dst.at[rows]
        return remote(dst if src is None else src, dst, h_send.at[c, kind], h_recv.at[c, kind], roll, to)

    sends = []

    def start(copy):
        copy.start()
        sends.append(copy)

    def landed(c, kind, block, rows=None):
        hop(c, kind, block, across, rows=rows).wait_recv()

    top_rows, low_rows = pl.ds(0, TOK // 2), pl.ds(TOK // 2, TOK // 2)
    far, far_across = pos(x + 2, y), pos(x + 2, 1 - y)
    left_across, right_across = pos(x - 1, 1 - y), pos(x + 1, 1 - y)
    along_y = (0, 1)
    along_x = (2, 3)

    for c in along_x + along_y:
        own = hidden.at[:, pl.ds(c * CHUNK, CHUNK)]
        start(hop(c, 0, tp, across, own))
        start(hop(c, 1, tp, right, own))
        start(hop(c, 2, tp, left, own))

    def pass_on(c):
        landed(c, 1, left)
        start(hop(c, 5, left, right, rows=top_rows))
        if c in along_x:
            start(hop(c, 3, left, across))
        landed(c, 2, right)
        start(hop(c, 6, right, left, rows=low_rows))
        if c in along_x:
            start(hop(c, 4, right, across))

    def spread(c):
        landed(c, 0, across)
        start(hop(c, 3, across, right))
        start(hop(c, 4, across, left))
        pass_on(c)

    def spread_again(c):
        landed(c, 3, left_across)
        start(hop(c, 7, left_across, right, rows=top_rows))
        landed(c, 4, right_across)
        start(hop(c, 8, right_across, left, rows=low_rows))

    def far_across_y(c):
        landed(c, 5, far, top_rows)
        landed(c, 6, far, low_rows)
        start(hop(c, 7, far, across))

    scale = 1.0 / math.sqrt(HD)
    row = lax.broadcasted_iota(jnp.int32, (QPK * GROUP, GROUP * CACHE), 0)
    col = lax.broadcasted_iota(jnp.int32, (QPK * GROUP, GROUP * CACHE), 1)
    same = (row % GROUP) == (col // CACHE)
    col_row = lax.broadcasted_iota(jnp.int32, (1, GROUP * CACHE), 1)

    def block_queries(g, t):
        at = pl.ds(pl.multiple_of(g * GROUP, GROUP), GROUP)
        return jnp.concatenate([queries[t, at, j * HD : (j + 1) * HD] for j in range(QPK)], axis=0)

    def cached(g, _):
        at = pl.ds(pl.multiple_of(g * GROUP, GROUP), GROUP)
        k = kbuf[at].reshape(GROUP * CACHE, HD)
        v = vbuf[at].reshape(GROUP * CACHE, HD)
        length = jnp.zeros((1, GROUP * CACHE), jnp.int32)
        for s in range(GROUP):
            length = jnp.where(col_row // CACHE == s, lens[g * GROUP + s], length)
        live = same & (col_row % CACHE < length)
        for t in range(STEPS):
            q = block_queries(g, t)
            scores = lax.dot_general(q, k, NT, preferred_element_type=jnp.float32) * scale
            scores = jnp.where(live, scores, NEG)
            top = jnp.max(scores, axis=1, keepdims=True)
            w = jnp.exp(scores - top)
            total = jnp.sum(w, axis=1, keepdims=True)
            mixed = jnp.dot(w.astype(jnp.bfloat16), v, preferred_element_type=jnp.float32)
            to = pl.ds(t * QPK * GROUP, QPK * GROUP)
            acc[g, to] = mixed
            top_ref[g, to] = jnp.broadcast_to(top, (QPK * GROUP, HD))
            sum_ref[g, to] = jnp.broadcast_to(total, (QPK * GROUP, HD))
        return 0

    for copy in loads[3:7]:
        copy.wait()
    lax.fori_loop(0, 2, cached, 0)
    for c in along_x:
        pass_on(c)
    lax.fori_loop(2, 4, cached, 0)
    for c in along_y:
        spread(c)
    pl.when(picks)(pick_z)
    for c in along_x:
        far_across_y(c)
    for c in along_y:
        spread_again(c)
    pl.when(picks)(pick_y)

    for copy in loads[7:]:
        copy.wait()
    projected = None
    for c in along_y + along_x:
        if c in along_y:
            landed(c, 5, far, top_rows)
            landed(c, 6, far, low_rows)
            landed(c, 7, far_across, top_rows)
            landed(c, 8, far_across, low_rows)
        else:
            landed(c, 0, across)
            landed(c, 3, left_across)
            landed(c, 4, right_across)
            landed(c, 7, far_across)
        part = jnp.dot(
            gathered[c].reshape(TP * TOK, CHUNK), weights[c * CHUNK : (c + 1) * CHUNK],
            preferred_element_type=jnp.float32,
        )
        projected = part if projected is None else projected + part

    for a in range(PICKERS):
        @pl.when(z != a)
        def _():
            remote(half.at[0], now.at[core, a], p3_send.at[0], p3_recv.at[a], twin, tp).wait_recv()
    p4 = remote(now.at[core], now.at[core], p4_send, p4_recv, twin, tp)
    p4.start()
    remote(now.at[1 - core], now.at[1 - core], p4_send, p4_recv, twin, tp).wait_recv()

    factors = now[...].reshape(2 * R, WIDTH)
    per = CHUNK // ROWS_TP
    mine_hidden = gathered[
        tp // per, :, :, pl.ds(pl.multiple_of(lax.rem(tp, per) * ROWS_TP, ROWS_TP), ROWS_TP)
    ].reshape(TP * TOK, ROWS_TP)
    low_all[tp] = lax.dot_general(
        mine_hidden, factors[:, :ROWS_TP], NT, preferred_element_type=jnp.float32
    ).astype(jnp.bfloat16)

    def all_to(d):
        q = lax.rem(tp + d, TP)
        return remote(low_all.at[tp], low_all.at[tp], g_send.at[q], g_recv.at[tp], roll, q)

    def all_from(d):
        q = lax.rem(tp + d, TP)
        return remote(low_all.at[q], low_all.at[q], g_send.at[q], g_recv.at[q], roll, q)

    for d in range(1, TP):
        all_to(d).start()
    zero = jnp.zeros((R, HD), jnp.bfloat16)
    up_both = jnp.concatenate(
        [
            jnp.concatenate([factors[:R, ROWS_TP:], zero], axis=0),
            jnp.concatenate([zero, factors[R:, ROWS_TP:]], axis=0),
        ],
        axis=1,
    )
    for d in range(1, TP):
        all_from(d).wait_recv()
    low = jnp.sum(low_all[...].astype(jnp.float32), axis=0).astype(jnp.bfloat16)
    projected = projected + jnp.dot(low, up_both, preferred_element_type=jnp.float32)
    fresh = projected.astype(jnp.bfloat16)

    span = GROUP * STEPS
    row2 = lax.broadcasted_iota(jnp.int32, (ROWS, span), 0)
    col2 = lax.broadcasted_iota(jnp.int32, (ROWS, span), 1)
    sample2 = col2 // TOK * (GROUP // 2) + col2 % (GROUP // 2)
    step2 = col2 % TOK // (GROUP // 2)
    live2 = (row2 % GROUP == sample2) & (step2 <= row2 // (QPK * GROUP))
    for g in range(GROUPS):
        q = jnp.concatenate([block_queries(g, t) for t in range(STEPS)], axis=0)
        k = fresh[g * span : (g + 1) * span, :HD]
        v = fresh[g * span : (g + 1) * span, HD:]
        scores = lax.dot_general(q, k, NT, preferred_element_type=jnp.float32) * scale
        scores = jnp.where(live2, scores, NEG)
        old_top = top_ref[g]
        top = jnp.maximum(old_top, jnp.max(scores, axis=1, keepdims=True))
        w = jnp.exp(scores - top[:, :span])
        fade = jnp.exp(old_top - top)
        total = sum_ref[g] * fade + jnp.sum(w, axis=1, keepdims=True)
        mixed = acc[g] * fade + jnp.dot(w.astype(jnp.bfloat16), v, preferred_element_type=jnp.float32)
        done = (mixed / total).astype(jnp.bfloat16)
        for t in range(STEPS):
            for j in range(QPK):
                at = (t * QPK + j) * GROUP
                out[t, g * GROUP : (g + 1) * GROUP, j * HD : (j + 1) * HD] = done[at : at + GROUP]

    for copy in p0 + sends + [p4]:
        copy.wait_send()
    for d in range(1, TP):
        all_to(d).wait_send()
    for a in range(PICKERS):
        @pl.when(z != a)
        def _():
            to_picker(a).wait_send()

    @pl.when(picks)
    def _():
        for d in range(1, YS):
            to_other_y(lax.rem(y_hi + d, YS)).wait_send()
        for d in range(1, ZS):
            to_column(lax.rem(z + d, ZS)).wait_send()


def local(hidden, queries, key_cache, value_cache, cache_len, base_key, base_value, factor_a, factor_b, owner):
    down = jnp.swapaxes(factor_a[0], 1, 2).reshape(2 * R, ROWS_TP)
    up = factor_b[0].reshape(2 * R, HD)
    hbm = pl.BlockSpec(memory_space=pltpu.HBM)
    dma = pltpu.SemaphoreType.DMA
    vmem, bf16, f32 = pltpu.VMEM, jnp.bfloat16, jnp.float32
    return pl.pallas_call(
        kernel,
        out_shape=pltpu.VMEM((STEPS, SAMP, QPK * HD), jnp.bfloat16),
        in_specs=[hbm] * 10,
        out_specs=pl.BlockSpec(memory_space=pltpu.VMEM),
        scratch_shapes=[
            pltpu.SMEM((2,), jnp.int32),
            pltpu.SMEM((SAMP,), jnp.int32),
            vmem((STEPS, SAMP, QPK * HD), bf16),
            vmem((2 * R, ROWS_TP), bf16),
            vmem((2 * R, HD), bf16),
            vmem((NC, TP, TOK, CHUNK), bf16),
            vmem((D, 2 * HD), bf16),
            vmem((SAMP, CACHE, HD), bf16),
            vmem((SAMP, CACHE, HD), bf16),
            vmem((R, WIDTH), bf16),
            vmem((PICKERS, PIECE, WIDTH), bf16),
            vmem((ZS, PIECE, WIDTH), bf16),
            vmem((YS, PIECE, WIDTH), bf16),
            vmem((2, PICKERS, PIECE, WIDTH), bf16),
            vmem((GROUPS, ROWS, HD), f32),
            vmem((GROUPS, ROWS, HD), f32),
            vmem((GROUPS, ROWS, HD), f32),
            vmem((TP, TP * TOK, 2 * R), bf16),
            dma((9 + NC,)),
            dma((2,)), dma((2,)),
            dma((PICKERS,)), dma((ZS,)),
            dma((YS,)), dma((YS,)),
            dma((ZS,)), dma((PICKERS,)),
            dma, dma,
            dma((NC, 9)), dma((NC, 9)),
            dma((TP,)), dma((TP,)),
        ],
        compiler_params=pltpu.CompilerParams(
            collective_id=0, has_side_effects=True, vmem_limit_bytes=60 * 1024 * 1024
        ),
    )(
        owner, cache_len, hidden.reshape(TOK, D), queries, key_cache, value_cache,
        base_key, base_value, down, up,
    )


def solution(mesh):
    placed = (
        P(None, ("roll", "tp"), None),
        P(None, "roll", "tp"),
        P("roll", None, "tp"),
        P("roll", None, "tp"),
        P("roll"),
        P(None, "tp"),
        P(None, "tp"),
        P("roll", None, "tp", None),
        P("roll", None, None, "tp"),
        P(),
    )
    return jax.shard_map(
        local, mesh=mesh, in_specs=placed, out_specs=P(None, "roll", "tp"), check_vma=False
    )
```

```python
import math

import jax
import jax.numpy as jnp
from jax import lax
from jax.experimental import pallas as pl
from jax.experimental.pallas import tpu as pltpu
from jax.sharding import PartitionSpec as P

D = 5120
HD = 128
QPK = 4
R = 64
STEPS = 4
SAMP = 64
CACHE = 32
TP = 8
ROWS_TP = D // TP
PIECE = 16
WIDTH = ROWS_TP + HD
NC = 4
CHUNK = D // NC
TOK = STEPS * SAMP // TP
ZS = 8
PICKERS = 4
YS = 4
LAST_Y = 2
GROUP = 16
GROUPS = SAMP // GROUP
ROWS = STEPS * QPK * GROUP
NEG = -1e30
MESH = pl.DeviceIdType.MESH
NT = (((1,), (1,)), ((), ()))
TN = (((0,), (0,)), ((), ()))


def kernel(
    owner_hbm, lens_hbm, hidden, queries_hbm, keys, values, base_key, base_value, down_hbm, up_hbm, out,
    owner, lens, queries, down, up,
    gathered, weights, kbuf, vbuf, other, half, bins_z, bins_y, now, acc, top_ref, sum_ref, low_all,
    load_sem, p0_send, p0_recv, p1_send, p1_recv, p2_send, p2_recv, p3_send, p3_recv, p4_send, p4_recv,
    h_send, h_recv, g_send, g_recv, go_z, go_y,
):
    roll, tp = lax.axis_index("roll"), lax.axis_index("tp")
    y_hi, z, core = roll // 16, roll // 2 % 8, roll % 2
    x, y = tp // 2, tp % 2
    pos = lambda px, py: lax.rem(px + 8, 4) * 2 + py
    right, left, across = pos(x + 1, y), pos(x - 1, y), pos(x, 1 - y)
    twin = roll + 1 - 2 * core
    picks = z < PICKERS

    def at_z(to_z):
        return y_hi * 16 + to_z * 2 + core

    def at_y(to_y):
        return to_y * 16 + z * 2 + core

    def remote(src, dst, send, recv, to_roll, to_tp):
        return pltpu.make_async_remote_copy(
            src_ref=src, dst_ref=dst, send_sem=send, recv_sem=recv,
            device_id=(to_roll, to_tp), device_id_type=MESH,
        )

    loads = [
        pltpu.make_async_copy(src, dst, load_sem.at[k])
        for k, (src, dst) in enumerate(
            [
                (down_hbm, down), (up_hbm, up), (owner_hbm, owner), (lens_hbm, lens), (queries_hbm, queries),
                (keys, kbuf), (values, vbuf),
                (base_key, weights.at[:, pl.ds(0, HD)]), (base_value, weights.at[:, pl.ds(HD, HD)]),
            ]
            + [(hidden.at[:, pl.ds(c * CHUNK, CHUNK)], gathered.at[c, tp]) for c in range(NC)]
        )
    ]
    for copy in loads:
        copy.start()

    barrier = pltpu.get_barrier_semaphore()
    tells_y = picks & (y_hi == LAST_Y)
    asks_y = picks & (y_hi != LAST_Y)

    def greet(to_roll, to_tp):
        pl.semaphore_signal(barrier, inc=1, device_id=(to_roll, to_tp), device_id_type=MESH)

    greet(twin, tp)
    for d in range(1, TP):
        greet(roll, lax.rem(tp + d, TP))

    @pl.when(picks)
    def _():
        for k in range(PICKERS, ZS):
            greet(at_z(k), tp)

    @pl.when(asks_y)
    def _():
        greet(at_y(LAST_Y), tp)

    pl.semaphore_wait(
        barrier, TP + jnp.where(picks, 0, PICKERS) + jnp.where(tells_y, YS - 1, 0)
    )

    @pl.when(z == PICKERS)
    def _():
        for k in range(PICKERS):
            pl.semaphore_signal(go_z, inc=1, device_id=(at_z(k), tp), device_id_type=MESH)

    @pl.when(tells_y)
    def _():
        for k in range(YS):
            if k != LAST_Y:
                pl.semaphore_signal(go_y, inc=1, device_id=(at_y(k), tp), device_id_type=MESH)

    mine = pl.ds(pl.multiple_of(core * R, R), R)
    theirs = pl.ds(pl.multiple_of((1 - core) * R, R), R)
    p0 = [
        remote(down_hbm.at[theirs], other.at[:, pl.ds(0, ROWS_TP)], p0_send.at[0], p0_recv.at[0], twin, tp),
        remote(up_hbm.at[theirs], other.at[:, pl.ds(ROWS_TP, HD)], p0_send.at[1], p0_recv.at[1], twin, tp),
    ]
    for copy in p0:
        copy.start()
    for copy in loads[:3]:
        copy.wait()
    owner_here = owner[core]
    for copy in p0:
        copy.wait_recv()
    kept = jnp.where(
        owner_here % 2 == core, jnp.concatenate([down[mine, :], up[mine, :]], axis=1), other[...]
    )
    half[...] = kept.reshape(PICKERS, PIECE, WIDTH)

    def to_picker(a):
        return remote(half.at[a], bins_z.at[z], p1_send.at[a], p1_recv.at[z], at_z(a), tp)

    @pl.when(jnp.logical_not(picks))
    def _():
        for a in range(PICKERS):
            to_picker(a).start()

    def pickers_pieces():
        pl.semaphore_wait(go_z, 1)
        for a in range(PICKERS):
            @pl.when(z != a)
            def _():
                to_picker(a).start()

            @pl.when(z == a)
            def _():
                bins_z[z] = half[a]

    def to_other_y(k):
        return remote(bins_y.at[y_hi], bins_y.at[y_hi], p2_send.at[k], p2_recv.at[y_hi], at_y(k), tp)

    def pick_z():
        for d in range(1, ZS):
            k = lax.rem(z + d, ZS)
            remote(half.at[0], bins_z.at[k], p1_send.at[0], p1_recv.at[k], twin, tp).wait_recv()
        bins_y[y_hi] = bins_z[owner_here // 2 % ZS]

        @pl.when(asks_y)
        def _():
            pl.semaphore_wait(go_y, 1)

        for k in range(YS):
            @pl.when(y_hi != k)
            def _():
                to_other_y(k).start()

    def to_column(k):
        return remote(now.at[core, z], now.at[core, z], p3_send.at[k], p3_recv.at[z], at_z(k), tp)

    def pick_y():
        for d in range(1, YS):
            k = lax.rem(y_hi + d, YS)
            remote(half.at[0], bins_y.at[k], p2_send.at[0], p2_recv.at[k], twin, tp).wait_recv()
        now[core, z] = bins_y[owner_here // 16]
        for k in range(ZS):
            @pl.when(z != k)
            def _():
                to_column(k).start()

    def hop(c, kind, block, to, src=None, rows=None):
        dst = gathered.at[c, block]
        if rows is not None:
            dst = dst.at[rows]
        return remote(dst if src is None else src, dst, h_send.at[c, kind], h_recv.at[c, kind], roll, to)

    sends = []

    def start(copy):
        copy.start()
        sends.append(copy)

    def landed(c, kind, block, rows=None):
        hop(c, kind, block, across, rows=rows).wait_recv()

    top_rows, low_rows = pl.ds(0, TOK // 2), pl.ds(TOK // 2, TOK // 2)
    far, far_across = pos(x + 2, y), pos(x + 2, 1 - y)
    left_across, right_across = pos(x - 1, 1 - y), pos(x + 1, 1 - y)
    along_y = (0, 1, 2)
    along_x = (3,)

    for c in along_x + along_y:
        own = hidden.at[:, pl.ds(c * CHUNK, CHUNK)]
        start(hop(c, 0, tp, across, own))
        start(hop(c, 1, tp, right, own))
        start(hop(c, 2, tp, left, own))

    def pass_on(c):
        landed(c, 1, left)
        start(hop(c, 5, left, right, rows=top_rows))
        if c in along_x:
            start(hop(c, 3, left, across))
        landed(c, 2, right)
        start(hop(c, 6, right, left, rows=low_rows))
        if c in along_x:
            start(hop(c, 4, right, across))

    def spread(c):
        landed(c, 0, across)
        start(hop(c, 3, across, right))
        start(hop(c, 4, across, left))
        pass_on(c)

    def spread_again(c):
        landed(c, 3, left_across)
        start(hop(c, 7, left_across, right, rows=top_rows))
        landed(c, 4, right_across)
        start(hop(c, 8, right_across, left, rows=low_rows))

    def far_across_y(c):
        landed(c, 5, far, top_rows)
        landed(c, 6, far, low_rows)
        start(hop(c, 7, far, across))

    scale = 1.0 / math.sqrt(HD)
    row = lax.broadcasted_iota(jnp.int32, (QPK * GROUP, GROUP * CACHE), 0)
    col = lax.broadcasted_iota(jnp.int32, (QPK * GROUP, GROUP * CACHE), 1)
    same = (row % GROUP) == (col // CACHE)
    col_row = lax.broadcasted_iota(jnp.int32, (1, GROUP * CACHE), 1)

    def block_queries(g, t):
        at = pl.ds(pl.multiple_of(g * GROUP, GROUP), GROUP)
        return jnp.concatenate([queries[t, at, j * HD : (j + 1) * HD] for j in range(QPK)], axis=0)

    def cached(g, _):
        at = pl.ds(pl.multiple_of(g * GROUP, GROUP), GROUP)
        k = kbuf[at].reshape(GROUP * CACHE, HD)
        v = vbuf[at].reshape(GROUP * CACHE, HD)
        length = jnp.zeros((1, GROUP * CACHE), jnp.int32)
        for s in range(GROUP):
            length = jnp.where(col_row // CACHE == s, lens[g * GROUP + s], length)
        live = same & (col_row % CACHE < length)
        for t in range(STEPS):
            q = block_queries(g, t)
            scores = lax.dot_general(q, k, NT, preferred_element_type=jnp.float32) * scale
            scores = jnp.where(live, scores, NEG)
            top = jnp.max(scores, axis=1, keepdims=True)
            w = jnp.exp(scores - top)
            total = jnp.sum(w, axis=1, keepdims=True)
            mixed = jnp.dot(w.astype(jnp.bfloat16), v, preferred_element_type=jnp.float32)
            to = pl.ds(t * QPK * GROUP, QPK * GROUP)
            acc[g, to] = mixed
            top_ref[g, to] = jnp.broadcast_to(top, (QPK * GROUP, HD))
            sum_ref[g, to] = jnp.broadcast_to(total, (QPK * GROUP, HD))
        return 0

    for copy in loads[3:7]:
        copy.wait()
    lax.fori_loop(0, 2, cached, 0)
    for c in along_x:
        pass_on(c)
    lax.fori_loop(2, 4, cached, 0)
    pl.when(picks)(pickers_pieces)
    for c in along_y:
        spread(c)
    pl.when(picks)(pick_z)
    for c in along_x:
        far_across_y(c)
    for c in along_y:
        spread_again(c)
    pl.when(picks)(pick_y)

    for copy in loads[7:]:
        copy.wait()
    for c in along_y:
        landed(c, 5, far, top_rows)
        landed(c, 6, far, low_rows)
        landed(c, 7, far_across, top_rows)
        landed(c, 8, far_across, low_rows)
    for c in along_x:
        landed(c, 0, across)
        landed(c, 3, left_across)
        landed(c, 4, right_across)
        landed(c, 7, far_across)

    for a in range(PICKERS):
        @pl.when(z != a)
        def _():
            remote(half.at[0], now.at[core, a], p3_send.at[0], p3_recv.at[a], twin, tp).wait_recv()
    p4 = remote(now.at[core], now.at[core], p4_send, p4_recv, twin, tp)
    p4.start()

    per = CHUNK // ROWS_TP
    mine_hidden = gathered[
        tp // per, :, :, pl.ds(pl.multiple_of(lax.rem(tp, per) * ROWS_TP, ROWS_TP), ROWS_TP)
    ].reshape(TP * TOK, ROWS_TP)

    def multiply(member):
        down_rows = now[member].reshape(R, WIDTH)[:, :ROWS_TP]
        low_all[member, tp] = lax.dot_general(
            down_rows, mine_hidden, NT, preferred_element_type=jnp.float32
        ).astype(jnp.bfloat16)

    def all_to(member, d):
        q = lax.rem(tp + d, TP)
        return remote(
            low_all.at[member, tp], low_all.at[member, tp], g_send.at[member, q], g_recv.at[member, tp], roll, q
        )

    def all_from(member, d):
        q = lax.rem(tp + d, TP)
        return remote(
            low_all.at[member, q], low_all.at[member, q], g_send.at[member, q], g_recv.at[member, q], roll, q
        )

    multiply(core)
    for d in range(1, TP):
        all_to(core, d).start()
    remote(now.at[1 - core], now.at[1 - core], p4_send, p4_recv, twin, tp).wait_recv()
    multiply(1 - core)
    for d in range(1, TP):
        all_to(1 - core, d).start()
    factors = now[...].reshape(2 * R, WIDTH)
    zero = jnp.zeros((R, HD), jnp.bfloat16)
    up_both = jnp.concatenate(
        [
            jnp.concatenate([factors[:R, ROWS_TP:], zero], axis=0),
            jnp.concatenate([zero, factors[R:, ROWS_TP:]], axis=0),
        ],
        axis=1,
    )

    projected = None
    for c in range(NC):
        part = jnp.dot(
            gathered[c].reshape(TP * TOK, CHUNK), weights[c * CHUNK : (c + 1) * CHUNK],
            preferred_element_type=jnp.float32,
        )
        projected = part if projected is None else projected + part

    for copy in p0 + sends + [p4]:
        copy.wait_send()
    for a in range(PICKERS):
        @pl.when(z != a)
        def _():
            to_picker(a).wait_send()

    @pl.when(picks)
    def _():
        for d in range(1, YS):
            to_other_y(lax.rem(y_hi + d, YS)).wait_send()
        for d in range(1, ZS):
            to_column(lax.rem(z + d, ZS)).wait_send()

    for member in range(2):
        for d in range(1, TP):
            all_from(member, d).wait_recv()
    low = jnp.sum(low_all[...].astype(jnp.float32), axis=1).astype(jnp.bfloat16).reshape(2 * R, TP * TOK)
    projected = projected + lax.dot_general(low, up_both, TN, preferred_element_type=jnp.float32)
    fresh = projected.astype(jnp.bfloat16)

    span = GROUP * STEPS
    row2 = lax.broadcasted_iota(jnp.int32, (ROWS, span), 0)
    col2 = lax.broadcasted_iota(jnp.int32, (ROWS, span), 1)
    sample2 = col2 // TOK * (GROUP // 2) + col2 % (GROUP // 2)
    step2 = col2 % TOK // (GROUP // 2)
    live2 = (row2 % GROUP == sample2) & (step2 <= row2 // (QPK * GROUP))
    for g in range(GROUPS):
        q = jnp.concatenate([block_queries(g, t) for t in range(STEPS)], axis=0)
        k = fresh[g * span : (g + 1) * span, :HD]
        v = fresh[g * span : (g + 1) * span, HD:]
        scores = lax.dot_general(q, k, NT, preferred_element_type=jnp.float32) * scale
        scores = jnp.where(live2, scores, NEG)
        old_top = top_ref[g]
        top = jnp.maximum(old_top, jnp.max(scores, axis=1, keepdims=True))
        w = jnp.exp(scores - top[:, :span])
        fade = jnp.exp(old_top - top)
        total = sum_ref[g] * fade + jnp.sum(w, axis=1, keepdims=True)
        mixed = acc[g] * fade + jnp.dot(w.astype(jnp.bfloat16), v, preferred_element_type=jnp.float32)
        done = (mixed / total).astype(jnp.bfloat16)
        for t in range(STEPS):
            for j in range(QPK):
                at = (t * QPK + j) * GROUP
                out[t, g * GROUP : (g + 1) * GROUP, j * HD : (j + 1) * HD] = done[at : at + GROUP]

    for member in range(2):
        for d in range(1, TP):
            all_to(member, d).wait_send()


def local(hidden, queries, key_cache, value_cache, cache_len, base_key, base_value, factor_a, factor_b, owner):
    down = jnp.swapaxes(factor_a[0], 1, 2).reshape(2 * R, ROWS_TP)
    up = factor_b[0].reshape(2 * R, HD)
    hbm = pl.BlockSpec(memory_space=pltpu.HBM)
    dma = pltpu.SemaphoreType.DMA
    vmem, bf16, f32 = pltpu.VMEM, jnp.bfloat16, jnp.float32
    return pl.pallas_call(
        kernel,
        out_shape=pltpu.VMEM((STEPS, SAMP, QPK * HD), jnp.bfloat16),
        in_specs=[hbm] * 10,
        out_specs=pl.BlockSpec(memory_space=pltpu.VMEM),
        scratch_shapes=[
            pltpu.SMEM((2,), jnp.int32),
            pltpu.SMEM((SAMP,), jnp.int32),
            vmem((STEPS, SAMP, QPK * HD), bf16),
            vmem((2 * R, ROWS_TP), bf16),
            vmem((2 * R, HD), bf16),
            vmem((NC, TP, TOK, CHUNK), bf16),
            vmem((D, 2 * HD), bf16),
            vmem((SAMP, CACHE, HD), bf16),
            vmem((SAMP, CACHE, HD), bf16),
            vmem((R, WIDTH), bf16),
            vmem((PICKERS, PIECE, WIDTH), bf16),
            vmem((ZS, PIECE, WIDTH), bf16),
            vmem((YS, PIECE, WIDTH), bf16),
            vmem((2, PICKERS, PIECE, WIDTH), bf16),
            vmem((GROUPS, ROWS, HD), f32),
            vmem((GROUPS, ROWS, HD), f32),
            vmem((GROUPS, ROWS, HD), f32),
            vmem((2, TP, R, TP * TOK), bf16),
            dma((9 + NC,)),
            dma((2,)), dma((2,)),
            dma((PICKERS,)), dma((ZS,)),
            dma((YS,)), dma((YS,)),
            dma((ZS,)), dma((PICKERS,)),
            dma, dma,
            dma((NC, 9)), dma((NC, 9)),
            dma((2, TP)), dma((2, TP)),
            pltpu.SemaphoreType.REGULAR, pltpu.SemaphoreType.REGULAR,
        ],
        compiler_params=pltpu.CompilerParams(
            collective_id=0, has_side_effects=True, vmem_limit_bytes=60 * 1024 * 1024
        ),
    )(
        owner, cache_len, hidden.reshape(TOK, D), queries, key_cache, value_cache,
        base_key, base_value, down, up,
    )


def solution(mesh):
    placed = (
        P(None, ("roll", "tp"), None),
        P(None, "roll", "tp"),
        P("roll", None, "tp"),
        P("roll", None, "tp"),
        P("roll"),
        P(None, "tp"),
        P(None, "tp"),
        P("roll", None, "tp", None),
        P("roll", None, None, "tp"),
        P(),
    )
    return jax.shard_map(
        local, mesh=mesh, in_specs=placed, out_specs=P(None, "roll", "tp"), check_vma=False
    )
```

```python
import math

import jax
import jax.numpy as jnp
from jax import lax
from jax.experimental import pallas as pl
from jax.experimental.pallas import tpu as pltpu
from jax.sharding import PartitionSpec as P

D = 5120
HD = 128
QPK = 4
R = 64
STEPS = 4
SAMP = 64
CACHE = 32
TP = 8
ROWS_TP = D // TP
PIECE = 16
WIDTH = ROWS_TP + HD
NC = 4
CHUNK = D // NC
TOK = STEPS * SAMP // TP
ZS = 8
PICKERS = 4
YS = 4
LAST_Y = 2
GROUP = 16
GROUPS = SAMP // GROUP
ROWS = STEPS * QPK * GROUP
NEG = -1e30
MESH = pl.DeviceIdType.MESH
NT = (((1,), (1,)), ((), ()))
TN = (((0,), (0,)), ((), ()))


def kernel(
    owner_hbm, lens_hbm, hidden, queries_hbm, keys, values, base_key, base_value, down_hbm, up_hbm, out,
    owner, lens, queries, down, up,
    gathered, weights, kbuf, vbuf, other, half, bins_z, bins_y, now, acc, top_ref, sum_ref, low_all,
    load_sem, p0_send, p0_recv, p1_send, p1_recv, p2_send, p2_recv, p3_send, p3_recv, p4_send, p4_recv,
    h_send, h_recv, g_send, g_recv, go_z, go_y,
):
    roll, tp = lax.axis_index("roll"), lax.axis_index("tp")
    y_hi, z, core = roll // 16, roll // 2 % 8, roll % 2
    x, y = tp // 2, tp % 2
    pos = lambda px, py: lax.rem(px + 8, 4) * 2 + py
    right, left, across = pos(x + 1, y), pos(x - 1, y), pos(x, 1 - y)
    twin = roll + 1 - 2 * core
    picks = z < PICKERS

    def at_z(to_z):
        return y_hi * 16 + to_z * 2 + core

    def at_y(to_y):
        return to_y * 16 + z * 2 + core

    def remote(src, dst, send, recv, to_roll, to_tp):
        return pltpu.make_async_remote_copy(
            src_ref=src, dst_ref=dst, send_sem=send, recv_sem=recv,
            device_id=(to_roll, to_tp), device_id_type=MESH,
        )

    loads = [
        pltpu.make_async_copy(src, dst, load_sem.at[k])
        for k, (src, dst) in enumerate(
            [
                (down_hbm, down), (up_hbm, up), (owner_hbm, owner), (lens_hbm, lens), (queries_hbm, queries),
                (keys, kbuf), (values, vbuf),
                (base_key, weights.at[:, pl.ds(0, HD)]), (base_value, weights.at[:, pl.ds(HD, HD)]),
            ]
            + [(hidden.at[:, pl.ds(c * CHUNK, CHUNK)], gathered.at[c, tp]) for c in range(NC)]
        )
    ]
    barrier = pltpu.get_barrier_semaphore()
    tells_y = picks & (y_hi == LAST_Y)
    asks_y = picks & (y_hi != LAST_Y)

    def greet(to_roll, to_tp):
        pl.semaphore_signal(barrier, inc=1, device_id=(to_roll, to_tp), device_id_type=MESH)

    greet(twin, tp)
    for d in range(1, TP):
        greet(roll, lax.rem(tp + d, TP))

    @pl.when(picks)
    def _():
        for k in range(PICKERS, ZS):
            greet(at_z(k), tp)

    @pl.when(asks_y)
    def _():
        greet(at_y(LAST_Y), tp)

    for copy in loads[:3]:
        copy.start()
    pl.semaphore_wait(
        barrier, TP + jnp.where(picks, 0, PICKERS) + jnp.where(tells_y, YS - 1, 0)
    )

    @pl.when(z == PICKERS)
    def _():
        for k in range(PICKERS):
            pl.semaphore_signal(go_z, inc=1, device_id=(at_z(k), tp), device_id_type=MESH)

    @pl.when(tells_y)
    def _():
        for k in range(YS):
            if k != LAST_Y:
                pl.semaphore_signal(go_y, inc=1, device_id=(at_y(k), tp), device_id_type=MESH)

    mine = pl.ds(pl.multiple_of(core * R, R), R)
    theirs = pl.ds(pl.multiple_of((1 - core) * R, R), R)
    p0 = [
        remote(down_hbm.at[theirs], other.at[:, pl.ds(0, ROWS_TP)], p0_send.at[0], p0_recv.at[0], twin, tp),
        remote(up_hbm.at[theirs], other.at[:, pl.ds(ROWS_TP, HD)], p0_send.at[1], p0_recv.at[1], twin, tp),
    ]
    for copy in p0:
        copy.start()
    for copy in loads[3:]:
        copy.start()
    for copy in loads[:3]:
        copy.wait()
    owner_here = owner[core]
    for copy in p0:
        copy.wait_recv()
    kept = jnp.where(
        owner_here % 2 == core, jnp.concatenate([down[mine, :], up[mine, :]], axis=1), other[...]
    )
    half[...] = kept.reshape(PICKERS, PIECE, WIDTH)

    def to_picker(a):
        return remote(half.at[a], bins_z.at[z], p1_send.at[a], p1_recv.at[z], at_z(a), tp)

    @pl.when(jnp.logical_not(picks))
    def _():
        for a in (1, 2, 0, 3):
            to_picker(a).start()

    def pickers_pieces():
        pl.semaphore_wait(go_z, 1)
        for a in range(PICKERS):
            @pl.when(z != a)
            def _():
                to_picker(a).start()

            @pl.when(z == a)
            def _():
                bins_z[z] = half[a]

    def to_other_y(k):
        return remote(bins_y.at[y_hi], bins_y.at[y_hi], p2_send.at[k], p2_recv.at[y_hi], at_y(k), tp)

    def pick_z():
        for d in range(1, ZS):
            k = lax.rem(z + d, ZS)
            remote(half.at[0], bins_z.at[k], p1_send.at[0], p1_recv.at[k], twin, tp).wait_recv()
        bins_y[y_hi] = bins_z[owner_here // 2 % ZS]

        @pl.when(asks_y)
        def _():
            pl.semaphore_wait(go_y, 1)

        for k in range(YS):
            @pl.when(y_hi != k)
            def _():
                to_other_y(k).start()

    def to_column(k):
        return remote(now.at[core, z], now.at[core, z], p3_send.at[k], p3_recv.at[z], at_z(k), tp)

    def pick_y():
        for d in range(1, YS):
            k = lax.rem(y_hi + d, YS)
            remote(half.at[0], bins_y.at[k], p2_send.at[0], p2_recv.at[k], twin, tp).wait_recv()
        now[core, z] = bins_y[owner_here // 16]
        for k in range(ZS):
            @pl.when(z != k)
            def _():
                to_column(k).start()

    def hop(c, kind, block, to, src=None, rows=None):
        dst = gathered.at[c, block]
        if rows is not None:
            dst = dst.at[rows]
        return remote(dst if src is None else src, dst, h_send.at[c, kind], h_recv.at[c, kind], roll, to)

    sends = []

    def start(copy):
        copy.start()
        sends.append(copy)

    def landed(c, kind, block, rows=None):
        hop(c, kind, block, across, rows=rows).wait_recv()

    top_rows, low_rows = pl.ds(0, TOK // 2), pl.ds(TOK // 2, TOK // 2)
    far, far_across = pos(x + 2, y), pos(x + 2, 1 - y)
    left_across, right_across = pos(x - 1, 1 - y), pos(x + 1, 1 - y)
    along_y = (0, 1, 2)
    along_x = (3,)

    for c in along_x + along_y:
        own = hidden.at[:, pl.ds(c * CHUNK, CHUNK)]
        start(hop(c, 0, tp, across, own))
        start(hop(c, 1, tp, right, own))
        start(hop(c, 2, tp, left, own))

    def pass_on(c):
        landed(c, 1, left)
        start(hop(c, 5, left, right, rows=top_rows))
        if c in along_x:
            start(hop(c, 3, left, across))
        landed(c, 2, right)
        start(hop(c, 6, right, left, rows=low_rows))
        if c in along_x:
            start(hop(c, 4, right, across))

    def spread(c):
        landed(c, 0, across)
        start(hop(c, 3, across, right))
        start(hop(c, 4, across, left))
        pass_on(c)

    def spread_again(c):
        landed(c, 3, left_across)
        start(hop(c, 7, left_across, right, rows=top_rows))
        landed(c, 4, right_across)
        start(hop(c, 8, right_across, left, rows=low_rows))

    def far_across_y(c):
        landed(c, 5, far, top_rows)
        landed(c, 6, far, low_rows)
        start(hop(c, 7, far, across))

    scale = 1.0 / math.sqrt(HD)
    row = lax.broadcasted_iota(jnp.int32, (QPK * GROUP, GROUP * CACHE), 0)
    col = lax.broadcasted_iota(jnp.int32, (QPK * GROUP, GROUP * CACHE), 1)
    same = (row % GROUP) == (col // CACHE)
    col_row = lax.broadcasted_iota(jnp.int32, (1, GROUP * CACHE), 1)

    def block_queries(g, t):
        at = pl.ds(pl.multiple_of(g * GROUP, GROUP), GROUP)
        return jnp.concatenate([queries[t, at, j * HD : (j + 1) * HD] for j in range(QPK)], axis=0)

    def cached(g, _):
        at = pl.ds(pl.multiple_of(g * GROUP, GROUP), GROUP)
        k = kbuf[at].reshape(GROUP * CACHE, HD)
        v = vbuf[at].reshape(GROUP * CACHE, HD)
        length = jnp.zeros((1, GROUP * CACHE), jnp.int32)
        for s in range(GROUP):
            length = jnp.where(col_row // CACHE == s, lens[g * GROUP + s], length)
        live = same & (col_row % CACHE < length)
        for t in range(STEPS):
            q = block_queries(g, t)
            scores = lax.dot_general(q, k, NT, preferred_element_type=jnp.float32) * scale
            scores = jnp.where(live, scores, NEG)
            top = jnp.max(scores, axis=1, keepdims=True)
            w = jnp.exp(scores - top)
            total = jnp.sum(w, axis=1, keepdims=True)
            mixed = jnp.dot(w.astype(jnp.bfloat16), v, preferred_element_type=jnp.float32)
            to = pl.ds(t * QPK * GROUP, QPK * GROUP)
            acc[g, to] = mixed
            top_ref[g, to] = jnp.broadcast_to(top, (QPK * GROUP, HD))
            sum_ref[g, to] = jnp.broadcast_to(total, (QPK * GROUP, HD))
        return 0

    for copy in loads[3:7]:
        copy.wait()
    lax.fori_loop(0, 2, cached, 0)
    for c in along_x:
        pass_on(c)
    lax.fori_loop(2, 4, cached, 0)
    spread(along_y[0])
    pl.when(picks)(pickers_pieces)
    for c in along_y[1:]:
        spread(c)
    pl.when(picks)(pick_z)
    for c in along_x:
        far_across_y(c)
    spread_again(along_y[0])
    pl.when(picks)(pick_y)
    for c in along_y[1:]:
        spread_again(c)

    for copy in loads[7:]:
        copy.wait()
    for c in along_y:
        landed(c, 5, far, top_rows)
        landed(c, 6, far, low_rows)
        landed(c, 7, far_across, top_rows)
        landed(c, 8, far_across, low_rows)
    for c in along_x:
        landed(c, 0, across)
        landed(c, 3, left_across)
        landed(c, 4, right_across)
        landed(c, 7, far_across)

    for a in range(PICKERS):
        @pl.when(z != a)
        def _():
            remote(half.at[0], now.at[core, a], p3_send.at[0], p3_recv.at[a], twin, tp).wait_recv()
    p4 = remote(now.at[core], now.at[core], p4_send, p4_recv, twin, tp)
    p4.start()

    per = CHUNK // ROWS_TP
    mine_hidden = gathered[
        tp // per, :, :, pl.ds(pl.multiple_of(lax.rem(tp, per) * ROWS_TP, ROWS_TP), ROWS_TP)
    ].reshape(TP * TOK, ROWS_TP)

    def multiply(member):
        down_rows = now[member].reshape(R, WIDTH)[:, :ROWS_TP]
        low_all[member, tp] = lax.dot_general(
            down_rows, mine_hidden, NT, preferred_element_type=jnp.float32
        ).astype(jnp.bfloat16)

    def all_to(member, d):
        q = lax.rem(tp + d, TP)
        return remote(
            low_all.at[member, tp], low_all.at[member, tp], g_send.at[member, q], g_recv.at[member, tp], roll, q
        )

    def all_from(member, d):
        q = lax.rem(tp + d, TP)
        return remote(
            low_all.at[member, q], low_all.at[member, q], g_send.at[member, q], g_recv.at[member, q], roll, q
        )

    multiply(core)
    for d in range(1, TP):
        all_to(core, d).start()
    remote(now.at[1 - core], now.at[1 - core], p4_send, p4_recv, twin, tp).wait_recv()
    multiply(1 - core)
    for d in range(1, TP):
        all_to(1 - core, d).start()
    factors = now[...].reshape(2 * R, WIDTH)
    zero = jnp.zeros((R, HD), jnp.bfloat16)
    up_both = jnp.concatenate(
        [
            jnp.concatenate([factors[:R, ROWS_TP:], zero], axis=0),
            jnp.concatenate([zero, factors[R:, ROWS_TP:]], axis=0),
        ],
        axis=1,
    )

    projected = None
    for c in range(NC):
        part = jnp.dot(
            gathered[c].reshape(TP * TOK, CHUNK), weights[c * CHUNK : (c + 1) * CHUNK],
            preferred_element_type=jnp.float32,
        )
        projected = part if projected is None else projected + part

    for copy in p0 + sends + [p4]:
        copy.wait_send()
    for a in range(PICKERS):
        @pl.when(z != a)
        def _():
            to_picker(a).wait_send()

    @pl.when(picks)
    def _():
        for d in range(1, YS):
            to_other_y(lax.rem(y_hi + d, YS)).wait_send()
        for d in range(1, ZS):
            to_column(lax.rem(z + d, ZS)).wait_send()

    for member in range(2):
        for d in range(1, TP):
            all_from(member, d).wait_recv()
    low = jnp.sum(low_all[...].astype(jnp.float32), axis=1).astype(jnp.bfloat16).reshape(2 * R, TP * TOK)
    projected = projected + lax.dot_general(low, up_both, TN, preferred_element_type=jnp.float32)
    fresh = projected.astype(jnp.bfloat16)

    span = GROUP * STEPS
    row2 = lax.broadcasted_iota(jnp.int32, (ROWS, span), 0)
    col2 = lax.broadcasted_iota(jnp.int32, (ROWS, span), 1)
    sample2 = col2 // TOK * (GROUP // 2) + col2 % (GROUP // 2)
    step2 = col2 % TOK // (GROUP // 2)
    live2 = (row2 % GROUP == sample2) & (step2 <= row2 // (QPK * GROUP))
    for g in range(GROUPS):
        q = jnp.concatenate([block_queries(g, t) for t in range(STEPS)], axis=0)
        k = fresh[g * span : (g + 1) * span, :HD]
        v = fresh[g * span : (g + 1) * span, HD:]
        scores = lax.dot_general(q, k, NT, preferred_element_type=jnp.float32) * scale
        scores = jnp.where(live2, scores, NEG)
        old_top = top_ref[g]
        top = jnp.maximum(old_top, jnp.max(scores, axis=1, keepdims=True))
        w = jnp.exp(scores - top[:, :span])
        fade = jnp.exp(old_top - top)
        total = sum_ref[g] * fade + jnp.sum(w, axis=1, keepdims=True)
        mixed = acc[g] * fade + jnp.dot(w.astype(jnp.bfloat16), v, preferred_element_type=jnp.float32)
        done = (mixed / total).astype(jnp.bfloat16)
        for t in range(STEPS):
            for j in range(QPK):
                at = (t * QPK + j) * GROUP
                out[t, g * GROUP : (g + 1) * GROUP, j * HD : (j + 1) * HD] = done[at : at + GROUP]

    for member in range(2):
        for d in range(1, TP):
            all_to(member, d).wait_send()


def local(hidden, queries, key_cache, value_cache, cache_len, base_key, base_value, factor_a, factor_b, owner):
    down = jnp.swapaxes(factor_a[0], 1, 2).reshape(2 * R, ROWS_TP)
    up = factor_b[0].reshape(2 * R, HD)
    hbm = pl.BlockSpec(memory_space=pltpu.HBM)
    dma = pltpu.SemaphoreType.DMA
    vmem, bf16, f32 = pltpu.VMEM, jnp.bfloat16, jnp.float32
    return pl.pallas_call(
        kernel,
        out_shape=pltpu.VMEM((STEPS, SAMP, QPK * HD), jnp.bfloat16),
        in_specs=[hbm] * 10,
        out_specs=pl.BlockSpec(memory_space=pltpu.VMEM),
        scratch_shapes=[
            pltpu.SMEM((2,), jnp.int32),
            pltpu.SMEM((SAMP,), jnp.int32),
            vmem((STEPS, SAMP, QPK * HD), bf16),
            vmem((2 * R, ROWS_TP), bf16),
            vmem((2 * R, HD), bf16),
            vmem((NC, TP, TOK, CHUNK), bf16),
            vmem((D, 2 * HD), bf16),
            vmem((SAMP, CACHE, HD), bf16),
            vmem((SAMP, CACHE, HD), bf16),
            vmem((R, WIDTH), bf16),
            vmem((PICKERS, PIECE, WIDTH), bf16),
            vmem((ZS, PIECE, WIDTH), bf16),
            vmem((YS, PIECE, WIDTH), bf16),
            vmem((2, PICKERS, PIECE, WIDTH), bf16),
            vmem((GROUPS, ROWS, HD), f32),
            vmem((GROUPS, ROWS, HD), f32),
            vmem((GROUPS, ROWS, HD), f32),
            vmem((2, TP, R, TP * TOK), bf16),
            dma((9 + NC,)),
            dma((2,)), dma((2,)),
            dma((PICKERS,)), dma((ZS,)),
            dma((YS,)), dma((YS,)),
            dma((ZS,)), dma((PICKERS,)),
            dma, dma,
            dma((NC, 9)), dma((NC, 9)),
            dma((2, TP)), dma((2, TP)),
            pltpu.SemaphoreType.REGULAR, pltpu.SemaphoreType.REGULAR,
        ],
        compiler_params=pltpu.CompilerParams(
            collective_id=0, has_side_effects=True, vmem_limit_bytes=60 * 1024 * 1024
        ),
    )(
        owner, cache_len, hidden.reshape(TOK, D), queries, key_cache, value_cache,
        base_key, base_value, down, up,
    )


def solution(mesh):
    placed = (
        P(None, ("roll", "tp"), None),
        P(None, "roll", "tp"),
        P("roll", None, "tp"),
        P("roll", None, "tp"),
        P("roll"),
        P(None, "tp"),
        P(None, "tp"),
        P("roll", None, "tp", None),
        P("roll", None, None, "tp"),
        P(),
    )
    return jax.shard_map(
        local, mesh=mesh, in_specs=placed, out_specs=P(None, "roll", "tp"), check_vma=False
    )
```

```python
import math

import jax
import jax.numpy as jnp
from jax import lax
from jax.experimental import pallas as pl
from jax.experimental.pallas import tpu as pltpu
from jax.sharding import PartitionSpec as P

D = 5120
HD = 128
QPK = 4
R = 64
STEPS = 4
SAMP = 64
CACHE = 32
TP = 8
ROWS_TP = D // TP
PIECE = 16
WIDTH = ROWS_TP + HD
NC = 4
CHUNK = D // NC
TOK = STEPS * SAMP // TP
ZS = 8
PICKERS = 4
YS = 4
LAST_Y = 2
GROUP = 16
GROUPS = SAMP // GROUP
ROWS = STEPS * QPK * GROUP
NEG = -1e30
MESH = pl.DeviceIdType.MESH
NT = (((1,), (1,)), ((), ()))
TN = (((0,), (0,)), ((), ()))


def kernel(
    owner_hbm, lens_hbm, hidden, queries_hbm, keys, values, base_key, base_value, down_hbm, up_hbm, out,
    owner, lens, queries, down, up,
    gathered, weights, kbuf, vbuf, other, half, bins_z, bins_y, now, acc, top_ref, sum_ref, low_all, stacked, live2,
    load_sem, p0_send, p0_recv, p1_send, p1_recv, p2_send, p2_recv, p3_send, p3_recv, p4_send, p4_recv,
    h_send, h_recv, g_send, g_recv, go_z, go_y,
):
    roll, tp = lax.axis_index("roll"), lax.axis_index("tp")
    y_hi, z, core = roll // 16, roll // 2 % 8, roll % 2
    x, y = tp // 2, tp % 2
    pos = lambda px, py: lax.rem(px + 8, 4) * 2 + py
    right, left, across = pos(x + 1, y), pos(x - 1, y), pos(x, 1 - y)
    twin = roll + 1 - 2 * core
    picks = z < PICKERS

    def at_z(to_z):
        return y_hi * 16 + to_z * 2 + core

    def at_y(to_y):
        return to_y * 16 + z * 2 + core

    def remote(src, dst, send, recv, to_roll, to_tp):
        return pltpu.make_async_remote_copy(
            src_ref=src, dst_ref=dst, send_sem=send, recv_sem=recv,
            device_id=(to_roll, to_tp), device_id_type=MESH,
        )

    loads = [
        pltpu.make_async_copy(src, dst, load_sem.at[k])
        for k, (src, dst) in enumerate(
            [
                (down_hbm, down), (up_hbm, up), (owner_hbm, owner), (lens_hbm, lens), (queries_hbm, queries),
                (keys, kbuf), (values, vbuf),
                (base_key, weights.at[:, pl.ds(0, HD)]), (base_value, weights.at[:, pl.ds(HD, HD)]),
            ]
            + [(hidden.at[:, pl.ds(c * CHUNK, CHUNK)], gathered.at[c, tp]) for c in range(NC)]
        )
    ]
    barrier = pltpu.get_barrier_semaphore()
    tells_y = picks & (y_hi == LAST_Y)
    asks_y = picks & (y_hi != LAST_Y)

    def greet(to_roll, to_tp):
        pl.semaphore_signal(barrier, inc=1, device_id=(to_roll, to_tp), device_id_type=MESH)

    greet(twin, tp)
    for d in range(1, TP):
        greet(roll, lax.rem(tp + d, TP))

    @pl.when(picks)
    def _():
        for k in range(PICKERS, ZS):
            greet(at_z(k), tp)

    @pl.when(asks_y)
    def _():
        greet(at_y(LAST_Y), tp)

    for copy in loads[:3]:
        copy.start()
    pl.semaphore_wait(
        barrier, TP + jnp.where(picks, 0, PICKERS) + jnp.where(tells_y, YS - 1, 0)
    )

    @pl.when(z == PICKERS)
    def _():
        for k in range(PICKERS):
            pl.semaphore_signal(go_z, inc=1, device_id=(at_z(k), tp), device_id_type=MESH)

    @pl.when(tells_y)
    def _():
        for k in range(YS):
            if k != LAST_Y:
                pl.semaphore_signal(go_y, inc=1, device_id=(at_y(k), tp), device_id_type=MESH)

    mine = pl.ds(pl.multiple_of(core * R, R), R)
    theirs = pl.ds(pl.multiple_of((1 - core) * R, R), R)
    p0 = [
        remote(down_hbm.at[theirs], other.at[:, pl.ds(0, ROWS_TP)], p0_send.at[0], p0_recv.at[0], twin, tp),
        remote(up_hbm.at[theirs], other.at[:, pl.ds(ROWS_TP, HD)], p0_send.at[1], p0_recv.at[1], twin, tp),
    ]
    for copy in p0:
        copy.start()
    for copy in loads[3:]:
        copy.start()
    for copy in loads[:3]:
        copy.wait()
    owner_here = owner[core]
    for copy in p0:
        copy.wait_recv()
    kept = jnp.where(
        owner_here % 2 == core, jnp.concatenate([down[mine, :], up[mine, :]], axis=1), other[...]
    )
    half[...] = kept.reshape(PICKERS, PIECE, WIDTH)

    def to_picker(a):
        return remote(half.at[a], bins_z.at[z], p1_send.at[a], p1_recv.at[z], at_z(a), tp)

    @pl.when(jnp.logical_not(picks))
    def _():
        for a in (1, 2, 0, 3):
            to_picker(a).start()

    def pickers_pieces():
        pl.semaphore_wait(go_z, 1)
        for a in range(PICKERS):
            @pl.when(z != a)
            def _():
                to_picker(a).start()

            @pl.when(z == a)
            def _():
                bins_z[z] = half[a]

    def to_other_y(k):
        return remote(bins_y.at[y_hi], bins_y.at[y_hi], p2_send.at[k], p2_recv.at[y_hi], at_y(k), tp)

    def pick_z():
        for d in range(1, ZS):
            k = lax.rem(z + d, ZS)
            remote(half.at[0], bins_z.at[k], p1_send.at[0], p1_recv.at[k], twin, tp).wait_recv()
        bins_y[y_hi] = bins_z[owner_here // 2 % ZS]

        @pl.when(asks_y)
        def _():
            pl.semaphore_wait(go_y, 1)

        for k in range(YS):
            @pl.when(y_hi != k)
            def _():
                to_other_y(k).start()

    def to_column(k):
        return remote(now.at[core, z], now.at[core, z], p3_send.at[k], p3_recv.at[z], at_z(k), tp)

    def pick_y():
        for d in range(1, YS):
            k = lax.rem(y_hi + d, YS)
            remote(half.at[0], bins_y.at[k], p2_send.at[0], p2_recv.at[k], twin, tp).wait_recv()
        now[core, z] = bins_y[owner_here // 16]
        for k in range(ZS):
            @pl.when(z != k)
            def _():
                to_column(k).start()

    def hop(c, kind, block, to, src=None, rows=None):
        dst = gathered.at[c, block]
        if rows is not None:
            dst = dst.at[rows]
        return remote(dst if src is None else src, dst, h_send.at[c, kind], h_recv.at[c, kind], roll, to)

    sends = []

    def start(copy):
        copy.start()
        sends.append(copy)

    def landed(c, kind, block, rows=None):
        hop(c, kind, block, across, rows=rows).wait_recv()

    top_rows, low_rows = pl.ds(0, TOK // 2), pl.ds(TOK // 2, TOK // 2)
    far, far_across = pos(x + 2, y), pos(x + 2, 1 - y)
    left_across, right_across = pos(x - 1, 1 - y), pos(x + 1, 1 - y)
    along_y = (0, 1, 2)
    along_x = (3,)

    for c in along_x + along_y:
        own = hidden.at[:, pl.ds(c * CHUNK, CHUNK)]
        start(hop(c, 0, tp, across, own))
        start(hop(c, 1, tp, right, own))
        start(hop(c, 2, tp, left, own))

    def pass_on(c):
        landed(c, 1, left)
        start(hop(c, 5, left, right, rows=top_rows))
        if c in along_x:
            start(hop(c, 3, left, across))
        landed(c, 2, right)
        start(hop(c, 6, right, left, rows=low_rows))
        if c in along_x:
            start(hop(c, 4, right, across))

    def spread(c):
        landed(c, 0, across)
        start(hop(c, 3, across, right))
        start(hop(c, 4, across, left))
        pass_on(c)

    def spread_again(c):
        landed(c, 3, left_across)
        start(hop(c, 7, left_across, right, rows=top_rows))
        landed(c, 4, right_across)
        start(hop(c, 8, right_across, left, rows=low_rows))

    def far_across_y(c):
        landed(c, 5, far, top_rows)
        landed(c, 6, far, low_rows)
        start(hop(c, 7, far, across))

    scale = 1.0 / math.sqrt(HD)
    row = lax.broadcasted_iota(jnp.int32, (QPK * GROUP, GROUP * CACHE), 0)
    col = lax.broadcasted_iota(jnp.int32, (QPK * GROUP, GROUP * CACHE), 1)
    same = (row % GROUP) == (col // CACHE)
    col_row = lax.broadcasted_iota(jnp.int32, (1, GROUP * CACHE), 1)

    def block_queries(g, t):
        at = pl.ds(pl.multiple_of(g * GROUP, GROUP), GROUP)
        return jnp.concatenate([queries[t, at, j * HD : (j + 1) * HD] for j in range(QPK)], axis=0)

    def cached(g, _):
        at = pl.ds(pl.multiple_of(g * GROUP, GROUP), GROUP)
        k = kbuf[at].reshape(GROUP * CACHE, HD)
        v = vbuf[at].reshape(GROUP * CACHE, HD)
        length = jnp.zeros((1, GROUP * CACHE), jnp.int32)
        for s in range(GROUP):
            length = jnp.where(col_row // CACHE == s, lens[g * GROUP + s], length)
        live = same & (col_row % CACHE < length)
        for t in range(STEPS):
            q = block_queries(g, t)
            stacked[g, pl.ds(t * QPK * GROUP, QPK * GROUP)] = q
            scores = lax.dot_general(q, k, NT, preferred_element_type=jnp.float32) * scale
            scores = jnp.where(live, scores, NEG)
            top = jnp.max(scores, axis=1, keepdims=True)
            w = jnp.exp(scores - top)
            total = jnp.sum(w, axis=1, keepdims=True)
            mixed = jnp.dot(w.astype(jnp.bfloat16), v, preferred_element_type=jnp.float32)
            to = pl.ds(t * QPK * GROUP, QPK * GROUP)
            acc[g, to] = mixed
            top_ref[g, to] = jnp.broadcast_to(top, (QPK * GROUP, HD))
            sum_ref[g, to] = jnp.broadcast_to(total, (QPK * GROUP, HD))
        return 0

    for copy in loads[3:7]:
        copy.wait()
    lax.fori_loop(0, 2, cached, 0)
    for c in along_x:
        pass_on(c)
    lax.fori_loop(2, 4, cached, 0)
    spread(along_y[0])
    pl.when(picks)(pickers_pieces)
    for c in along_y[1:]:
        spread(c)
    pl.when(picks)(pick_z)
    for c in along_x:
        far_across_y(c)
    spread_again(along_y[0])
    pl.when(picks)(pick_y)
    for c in along_y[1:]:
        spread_again(c)

    for copy in loads[7:]:
        copy.wait()
    for c in along_y:
        landed(c, 5, far, top_rows)
        landed(c, 6, far, low_rows)
        landed(c, 7, far_across, top_rows)
        landed(c, 8, far_across, low_rows)
    for c in along_x:
        landed(c, 0, across)
        landed(c, 3, left_across)
        landed(c, 4, right_across)
        landed(c, 7, far_across)

    for a in range(PICKERS):
        @pl.when(z != a)
        def _():
            remote(half.at[0], now.at[core, a], p3_send.at[0], p3_recv.at[a], twin, tp).wait_recv()
    p4 = remote(now.at[core], now.at[core], p4_send, p4_recv, twin, tp)
    p4.start()

    per = CHUNK // ROWS_TP
    mine_hidden = gathered[
        tp // per, :, :, pl.ds(pl.multiple_of(lax.rem(tp, per) * ROWS_TP, ROWS_TP), ROWS_TP)
    ].reshape(TP * TOK, ROWS_TP)

    def multiply(member):
        down_rows = now[member].reshape(R, WIDTH)[:, :ROWS_TP]
        low_all[member, tp] = lax.dot_general(
            down_rows, mine_hidden, NT, preferred_element_type=jnp.float32
        ).astype(jnp.bfloat16)

    def all_to(member, d):
        q = lax.rem(tp + d, TP)
        return remote(
            low_all.at[member, tp], low_all.at[member, tp], g_send.at[member, q], g_recv.at[member, tp], roll, q
        )

    def all_from(member, d):
        q = lax.rem(tp + d, TP)
        return remote(
            low_all.at[member, q], low_all.at[member, q], g_send.at[member, q], g_recv.at[member, q], roll, q
        )

    multiply(core)
    for d in range(1, TP):
        all_to(core, d).start()
    remote(now.at[1 - core], now.at[1 - core], p4_send, p4_recv, twin, tp).wait_recv()
    multiply(1 - core)
    for d in range(1, TP):
        all_to(1 - core, d).start()
    factors = now[...].reshape(2 * R, WIDTH)
    zero = jnp.zeros((R, HD), jnp.bfloat16)
    up_both = jnp.concatenate(
        [
            jnp.concatenate([factors[:R, ROWS_TP:], zero], axis=0),
            jnp.concatenate([zero, factors[R:, ROWS_TP:]], axis=0),
        ],
        axis=1,
    )

    projected = None
    for c in range(NC):
        part = jnp.dot(
            gathered[c].reshape(TP * TOK, CHUNK), weights[c * CHUNK : (c + 1) * CHUNK],
            preferred_element_type=jnp.float32,
        )
        projected = part if projected is None else projected + part

    span = GROUP * STEPS
    row2 = lax.broadcasted_iota(jnp.int32, (ROWS, span), 0)
    col2 = lax.broadcasted_iota(jnp.int32, (ROWS, span), 1)
    sample2 = col2 // TOK * (GROUP // 2) + col2 % (GROUP // 2)
    step2 = col2 % TOK // (GROUP // 2)
    live2[...] = jnp.where((row2 % GROUP == sample2) & (step2 <= row2 // (QPK * GROUP)), 0.0, NEG)

    for copy in p0 + sends + [p4]:
        copy.wait_send()
    for a in range(PICKERS):
        @pl.when(z != a)
        def _():
            to_picker(a).wait_send()

    @pl.when(picks)
    def _():
        for d in range(1, YS):
            to_other_y(lax.rem(y_hi + d, YS)).wait_send()
        for d in range(1, ZS):
            to_column(lax.rem(z + d, ZS)).wait_send()

    for member in range(2):
        for d in range(1, TP):
            all_from(member, d).wait_recv()
    low = jnp.sum(low_all[...].astype(jnp.float32), axis=1).astype(jnp.bfloat16).reshape(2 * R, TP * TOK)
    projected = projected + lax.dot_general(low, up_both, TN, preferred_element_type=jnp.float32)
    fresh = projected.astype(jnp.bfloat16)

    for g in range(GROUPS):
        q = stacked[g]
        k = fresh[g * span : (g + 1) * span, :HD]
        v = fresh[g * span : (g + 1) * span, HD:]
        scores = lax.dot_general(q, k, NT, preferred_element_type=jnp.float32) * scale
        scores = scores + live2[...]
        old_top = top_ref[g]
        top = jnp.maximum(old_top, jnp.max(scores, axis=1, keepdims=True))
        w = jnp.exp(scores - top[:, :span])
        fade = jnp.exp(old_top - top)
        total = sum_ref[g] * fade + jnp.sum(w, axis=1, keepdims=True)
        mixed = acc[g] * fade + jnp.dot(w.astype(jnp.bfloat16), v, preferred_element_type=jnp.float32)
        done = (mixed / total).astype(jnp.bfloat16)
        for t in range(STEPS):
            for j in range(QPK):
                at = (t * QPK + j) * GROUP
                out[t, g * GROUP : (g + 1) * GROUP, j * HD : (j + 1) * HD] = done[at : at + GROUP]

    for member in range(2):
        for d in range(1, TP):
            all_to(member, d).wait_send()


def local(hidden, queries, key_cache, value_cache, cache_len, base_key, base_value, factor_a, factor_b, owner):
    down = jnp.swapaxes(factor_a[0], 1, 2).reshape(2 * R, ROWS_TP)
    up = factor_b[0].reshape(2 * R, HD)
    hbm = pl.BlockSpec(memory_space=pltpu.HBM)
    dma = pltpu.SemaphoreType.DMA
    vmem, bf16, f32 = pltpu.VMEM, jnp.bfloat16, jnp.float32
    return pl.pallas_call(
        kernel,
        out_shape=pltpu.VMEM((STEPS, SAMP, QPK * HD), jnp.bfloat16),
        in_specs=[hbm] * 10,
        out_specs=pl.BlockSpec(memory_space=pltpu.VMEM),
        scratch_shapes=[
            pltpu.SMEM((2,), jnp.int32),
            pltpu.SMEM((SAMP,), jnp.int32),
            vmem((STEPS, SAMP, QPK * HD), bf16),
            vmem((2 * R, ROWS_TP), bf16),
            vmem((2 * R, HD), bf16),
            vmem((NC, TP, TOK, CHUNK), bf16),
            vmem((D, 2 * HD), bf16),
            vmem((SAMP, CACHE, HD), bf16),
            vmem((SAMP, CACHE, HD), bf16),
            vmem((R, WIDTH), bf16),
            vmem((PICKERS, PIECE, WIDTH), bf16),
            vmem((ZS, PIECE, WIDTH), bf16),
            vmem((YS, PIECE, WIDTH), bf16),
            vmem((2, PICKERS, PIECE, WIDTH), bf16),
            vmem((GROUPS, ROWS, HD), f32),
            vmem((GROUPS, ROWS, HD), f32),
            vmem((GROUPS, ROWS, HD), f32),
            vmem((2, TP, R, TP * TOK), bf16),
            vmem((GROUPS, ROWS, HD), bf16),
            vmem((ROWS, GROUP * STEPS), f32),
            dma((9 + NC,)),
            dma((2,)), dma((2,)),
            dma((PICKERS,)), dma((ZS,)),
            dma((YS,)), dma((YS,)),
            dma((ZS,)), dma((PICKERS,)),
            dma, dma,
            dma((NC, 9)), dma((NC, 9)),
            dma((2, TP)), dma((2, TP)),
            pltpu.SemaphoreType.REGULAR, pltpu.SemaphoreType.REGULAR,
        ],
        compiler_params=pltpu.CompilerParams(
            collective_id=0, has_side_effects=True, vmem_limit_bytes=60 * 1024 * 1024
        ),
    )(
        owner, cache_len, hidden.reshape(TOK, D), queries, key_cache, value_cache,
        base_key, base_value, down, up,
    )


def solution(mesh):
    placed = (
        P(None, ("roll", "tp"), None),
        P(None, "roll", "tp"),
        P("roll", None, "tp"),
        P("roll", None, "tp"),
        P("roll"),
        P(None, "tp"),
        P(None, "tp"),
        P("roll", None, "tp", None),
        P("roll", None, None, "tp"),
        P(),
    )
    return jax.shard_map(
        local, mesh=mesh, in_specs=placed, out_specs=P(None, "roll", "tp"), check_vma=False
    )
```
